32 devices in a mesh: view: 2 (over core), row: 4 (over y, x), feat: 4 (over z).
Axes of the slice: x: 2, y: 2, z: 4, core: 2. Of those that a mesh axis runs over, the one named last changes fastest.
Arguments:
- views: bfloat16 [2, 12288, 4096], P('view', ('row', 'feat')), may hold values from -8 to 8
- weights: float32 [2, 4096, 256], P('view', ('row', 'feat')), may hold values from -6 to 6
Outputs:
- new_weights: float32 [2, 4096, 256], P('view', ('row', 'feat'))
- projected: bfloat16 [2, 12288, 256], P('view', ('row', 'feat'))
The draws below stay inside these ranges and needn't reach their ends.
All inputs are finite; a program needn't handle non-finite values.
Results may differ from the reference program's by a relative error of at most 0.012.
Values may be sent and summed in bfloat16 or wider, within the bound.
No kernel may reach another device: no remote copies, remote signals or barrier semaphores. Data moves between devices by JAX's collectives and lax.ppermute only.
A program may use at most 64 MiB of HBM per device.

```python
import math
import jax
import jax.numpy as jnp
from jax import lax

D = 4096
K = 256
ITERS = 2
ROWS_DEV = 768
N = 12288


def draw_views(key, part):
    key = jax.random.fold_in(key, 11)
    keys = jax.random.split(key, 9)
    band_high = 0.5 * math.pi
    spread = 0.7
    noise = jax.random.normal(keys[7], (2, N, D), jnp.float32)
    omega = band_high * jax.random.uniform(keys[2], (N, 2), jnp.float32)
    phase = jax.random.uniform(keys[3], (N, 2), jnp.float32, -math.pi, math.pi)
    gains = jax.random.normal(keys[4], (N, 2), jnp.float32)
    block_amp = jnp.exp(jax.random.uniform(keys[5], (N // ROWS_DEV,), jnp.float32, -spread, spread))
    row_amp = jnp.repeat(block_amp, ROWS_DEV)
    feat_scale = jnp.exp(jax.random.uniform(keys[6], (2, D), jnp.float32, math.log(0.5), math.log(2.0)))
    stacked = []
    for view_index in range(2):
        placing = jax.random.permutation(keys[view_index], D).astype(jnp.float32)
        latent = gains[:, 0:1] * jnp.cos(omega[:, 0:1] * placing[None, :] + phase[:, 0:1])
        latent = latent + gains[:, 1:2] * jnp.cos(omega[:, 1:2] * placing[None, :] + phase[:, 1:2])
        single = feat_scale[view_index][None, :] * (row_amp[:, None] * latent + 0.5 * noise[view_index])
        stacked.append(jnp.clip(single, -8.0, 8.0))
    return jnp.stack(stacked).astype(jnp.bfloat16)


def level_of(own_key, extent, pieces, least, high):
    def one(position, parts):
        draws = jax.random.uniform(jax.random.fold_in(jax.random.fold_in(own_key, 6), position), (parts,), jnp.float32, least / len(pieces), high / len(pieces))
        return jnp.repeat(jnp.exp(draws), extent[position] // parts).reshape((-1,) + (1,) * (len(extent) - position - 1))

    gain = one(*pieces[0])
    for cut in pieces[1:]:
        gain = gain * one(*cut)
    return gain


def centred(own_key, dims, width, bound, pieces=(), kind=jnp.bfloat16):
    level = level_of(own_key, dims, pieces, -0.22, 0.18) if pieces else 1.0
    values = jax.random.normal(own_key, dims, jnp.float32) * width * level
    return jnp.minimum(jnp.maximum(values, -bound), bound).astype(kind)


def setup_inputs(seed: int = 0) -> dict:
    key_of = jax.random.split(jax.random.key(seed), 3)
    return {
        "views": draw_views(jax.random.fold_in(key_of[2], 71), 0),
        "weights": centred(key_of[1], (2, D, K), 1.0, 6.0, ((0, 2), (1, 16)), jnp.float32),
    }


epsilon = 1e-06
step_rate = 0.5

def reference(views, weights):
    iterate = [weights[0], weights[1]]
    projected = []
    for sweep in range(ITERS):
        scaling = []
        projected = []
        for view_index in range(2):
            summed_proj = jnp.dot(views[view_index], iterate[view_index].astype(jnp.bfloat16), preferred_element_type=jnp.float32)
            col_scale = lax.rsqrt(lax.optimization_barrier(jnp.mean(summed_proj * summed_proj, axis=0)) + epsilon)
            scaling.append(col_scale)
            projected.append((summed_proj * col_scale).astype(jnp.bfloat16))
        updated = []
        for view_index in range(2):
            residue = (projected[view_index].astype(jnp.float32) - projected[1 - view_index].astype(jnp.float32)).astype(jnp.bfloat16)
            grad_total = lax.dot_general(views[view_index], residue, (((0,), (0,)), ((), ())), preferred_element_type=jnp.float32) / N
            updated.append(math.sqrt(D) * (iterate[view_index] * scaling[view_index] - step_rate * grad_total))
        iterate = updated
    return (jnp.stack(iterate), jnp.stack(projected))
```

```python
import math

import jax
import jax.numpy as jnp
from jax import lax
from jax.experimental import pallas as pl
from jax.experimental.pallas import tpu as pltpu
from jax.sharding import PartitionSpec as P

ITERS = 2


epsilon = 1e-06
step_rate = 0.5


def xor_move(block, axis, mask):
    count = lax.axis_size(axis)
    return lax.ppermute(block, axis, [(i, i ^ mask) for i in range(count)])


def after(value, *others):
    return lax.optimization_barrier((value,) + others)[0]


def total(values):
    for axis in ("row", "feat"):
        own = values
        for mask in reversed(range(1, lax.axis_size(axis))):
            values = lax.optimization_barrier(values + xor_move(own, axis, mask))
    return values


def join(*blocks):
    return jnp.concatenate(blocks, axis=0)


def split(pair):
    deep = pair.shape[0] // 2
    return pair[:deep], pair[deep:]


ARRIVALS = (
    ((0, 0), (1, 0), (2, 0), (3, 0), (0, 1), (0, 2)),
    ((0, 3), (3, 2), (1, 1), (1, 2), (2, 1), (2, 2)),
    ((3, 1), (3, 3), (1, 3), (2, 3)),
)


def gather(own):
    b = {(0, 0): own}
    b[0, 2] = xor_move(own, "feat", 2)
    b[0, 1] = xor_move(own, "feat", 1)
    for r in (3, 1, 2):
        b[r, 0] = xor_move(own, "row", r)
    b[3, 2] = xor_move(b[0, 2], "row", 3)
    b[0, 3] = xor_move(b[0, 2], "feat", 1)
    for r in (1, 2):
        b[r, 1], b[r, 2] = split(xor_move(join(b[0, 1], b[0, 2]), "row", r))
    b[3, 1], b[3, 3] = split(xor_move(join(b[3, 0], b[3, 2]), "feat", 1))
    for r in (1, 2):
        b[r, 3] = xor_move(b[0, 3], "row", r)
    return b


def scatter(b):
    def send(axis, mask, *blocks):
        half = [block.astype(jnp.bfloat16) for block in blocks]
        got = xor_move(half[0] if len(half) == 1 else join(*half), axis, mask)
        return [part.astype(jnp.float32) for part in (split(got) if len(half) > 1 else [got])]

    def summed(first, *others):
        return lax.optimization_barrier(sum(others, first).astype(jnp.bfloat16))

    near_across, far_across = send("feat", 1, b[3, 1], b[3, 3])
    (left,), (right,) = send("row", 1, b[1, 3]), send("row", 2, b[2, 3])
    ones, twos = zip(*[send("row", r, b[r, 1], b[r, 2]) for r in (1, 2)])
    far_across = summed(b[3, 2], far_across)
    three = summed(after(b[0, 3], far_across), left, right)
    near_across = summed(after(b[3, 0], three), near_across)
    (far_across,), (three,) = send("row", 3, far_across), send("feat", 1, three)
    two = summed(b[0, 2], *twos, far_across, three)
    one = summed(after(b[0, 1], two), *ones)
    (two,), (near_across,), (one,) = (
        send("feat", 2, two),
        send("row", 3, near_across),
        send("feat", 1, one),
    )
    near = b[0, 0] + send("row", 1, b[1, 0])[0] + send("row", 2, b[2, 0])[0]
    return near + near_across + one + two


def any_mesh(samples, own_rows):
    row_total = samples.shape[0] * lax.axis_size("row") * lax.axis_size("feat")
    width_root = math.sqrt(samples.shape[1])
    for sweep in range(ITERS):
        dirs = lax.all_gather(
            own_rows.astype(jnp.bfloat16), ("row", "feat"), axis=0, tiled=True
        )
        summed_proj = jnp.dot(samples, dirs, preferred_element_type=jnp.float32)
        squares = lax.psum(jnp.sum(summed_proj * summed_proj, axis=0), ("row", "feat"))
        scaling = lax.rsqrt(squares / row_total + epsilon)
        own_proj = (summed_proj * scaling).astype(jnp.bfloat16)
        partner_proj = xor_move(own_proj, "view", 1)
        residue = (own_proj.astype(jnp.float32) - partner_proj.astype(jnp.float32)).astype(
            jnp.bfloat16
        )
        share = lax.dot_general(
            samples, residue, (((0,), (0,)), ((), ())), preferred_element_type=jnp.float32
        )
        share = lax.psum_scatter(share, ("row", "feat"), scatter_dimension=0, tiled=True)
        own_rows = width_root * (own_rows * scaling - step_rate * (share / row_total))
    return (own_rows[None], own_proj[None])


def regroup(samples, depth):
    rows_here = samples.shape[0]
    feats = lax.axis_size("feat")
    count = sum(len(places) for places in ARRIVALS)

    def kernel(samples_ref, *refs):
        outs, done = refs[:-1], refs[-1]
        row_at, feat_at = lax.axis_index("row"), lax.axis_index("feat")
        copies = []
        for out, places in zip(outs, ARRIVALS):
            for i, (r, t) in enumerate(places):
                start = pl.multiple_of(((row_at ^ r) * feats + (feat_at ^ t)) * depth, depth)
                copies.append(
                    pltpu.make_async_copy(
                        samples_ref.at[:, pl.ds(start, depth)],
                        out.at[:, pl.ds(i * depth, depth)],
                        done.at[len(copies)],
                    )
                )
                copies[-1].start()
        for copy in copies:
            copy.wait()

    return pl.pallas_call(
        kernel,
        out_shape=[
            jax.ShapeDtypeStruct((rows_here, len(places) * depth), samples.dtype)
            for places in ARRIVALS
        ],
        in_specs=[pl.BlockSpec(memory_space=pl.ANY)],
        out_specs=[pl.BlockSpec(memory_space=pl.ANY) for places in ARRIVALS],
        scratch_shapes=[pltpu.SemaphoreType.DMA((count,))],
        compiler_params=pltpu.CompilerParams(vmem_limit_bytes=1 << 20),
        cost_estimate=pl.CostEstimate(
            flops=0, bytes_accessed=2 * samples.size * 2, transcendentals=0
        ),
        name="regroup",
    )(samples)


def on_device(views, weights):
    samples = views[0]
    own_rows = weights[0]
    rows_here, width = samples.shape
    depth, pairs = own_rows.shape
    rows, feats = lax.axis_size("row"), lax.axis_size("feat")
    if (rows, feats) != (4, 4) or depth % 128:
        return any_mesh(samples, own_rows)
    row_total = rows_here * rows * feats
    width_root = math.sqrt(width)
    groups = regroup(samples, depth)
    for sweep in range(ITERS):
        dirs = gather(own_rows.astype(jnp.bfloat16))
        summed_proj = 0.0
        for g, places in enumerate(ARRIVALS):
            blocks = lax.optimization_barrier([dirs[p] for p in places])
            part = jnp.dot(
                groups[g], join(*blocks), preferred_element_type=jnp.float32
            )
            summed_proj = lax.optimization_barrier(summed_proj + part) if g < 2 else summed_proj + part
        kept_proj = lax.optimization_barrier(summed_proj.astype(jnp.bfloat16))
        partner_proj = xor_move(kept_proj, "view", 1).astype(jnp.float32)
        squares = jnp.sum(summed_proj * summed_proj, axis=0)
        scaling = lax.rsqrt(total(squares) / row_total + epsilon)
        partner_scaling = xor_move(scaling, "view", 1)
        own_proj = (kept_proj.astype(jnp.float32) * scaling).astype(jnp.bfloat16)
        partner_proj = (partner_proj * partner_scaling).astype(jnp.bfloat16)
        residue = (own_proj.astype(jnp.float32) - partner_proj.astype(jnp.float32)).astype(
            jnp.bfloat16
        )
        shares = {}
        for g in (2, 1, 0):
            share = lax.dot_general(
                groups[g], residue, (((0,), (0,)), ((), ())), preferred_element_type=jnp.float32
            )
            for i, place in enumerate(ARRIVALS[g]):
                shares[place] = share[i * depth : (i + 1) * depth]
        if sweep == ITERS - 1:
            kept_proj, shown_scaling = lax.optimization_barrier((kept_proj, scaling))
            own_proj = (kept_proj.astype(jnp.float32) * shown_scaling).astype(jnp.bfloat16)
        grad = scatter(shares) / row_total
        own_rows = width_root * (own_rows * scaling - step_rate * grad)
    return (own_rows[None], own_proj[None])


def solution(mesh):
    in_specs = (P("view", ("row", "feat"), None), P("view", ("row", "feat"), None))
    out_specs = (P("view", ("row", "feat"), None), P("view", ("row", "feat"), None))
    return jax.shard_map(
        on_device, mesh=mesh, in_specs=in_specs, out_specs=out_specs, check_vma=False
    )
```

```python
import math

import jax
import jax.numpy as jnp
from jax import lax
from jax.experimental import pallas as pl
from jax.experimental.pallas import tpu as pltpu
from jax.sharding import PartitionSpec as P

ITERS = 2


epsilon = 1e-06
step_rate = 0.5


def xor_move(block, axis, mask):
    count = lax.axis_size(axis)
    return lax.ppermute(block, axis, [(i, i ^ mask) for i in range(count)])


def after(value, *others):
    return lax.optimization_barrier((value,) + others)[0]


def total(values):
    for axis in ("row", "feat"):
        own = values
        for mask in reversed(range(1, lax.axis_size(axis))):
            values = lax.optimization_barrier(values + xor_move(own, axis, mask))
    return values


def join(*blocks):
    return jnp.concatenate(blocks, axis=0)


def split(pair):
    deep = pair.shape[0] // 2
    return pair[:deep], pair[deep:]


ARRIVALS = (
    ((0, 0), (1, 0), (2, 0), (3, 0), (0, 1), (0, 2)),
    ((0, 3), (3, 2), (1, 1), (1, 2), (2, 1), (2, 2)),
    ((3, 1), (3, 3), (1, 3), (2, 3)),
)


def gather(own):
    b = {(0, 0): own}
    b[0, 2] = xor_move(own, "feat", 2)
    b[0, 1] = xor_move(own, "feat", 1)
    for r in (3, 1, 2):
        b[r, 0] = xor_move(own, "row", r)
    b[3, 2] = xor_move(b[0, 2], "row", 3)
    b[0, 3] = xor_move(b[0, 2], "feat", 1)
    for r in (1, 2):
        pair = join(after(b[0, 1], b[3, 0]), b[0, 2])
        b[r, 1], b[r, 2] = split(xor_move(pair, "row", r))
    b[3, 1], b[3, 3] = split(xor_move(join(b[3, 0], b[3, 2]), "feat", 1))
    for r in (1, 2):
        b[r, 3] = xor_move(b[0, 3], "row", r)
    return b


def scatter(b):
    def send(axis, mask, *blocks):
        half = [block.astype(jnp.bfloat16) for block in blocks]
        got = xor_move(half[0] if len(half) == 1 else join(*half), axis, mask)
        return [part.astype(jnp.float32) for part in (split(got) if len(half) > 1 else [got])]

    def summed(first, *others):
        return lax.optimization_barrier(sum(others, first).astype(jnp.bfloat16))

    near_across, far_across = send("feat", 1, b[3, 1], b[3, 3])
    (left,), (right,) = send("row", 1, b[1, 3]), send("row", 2, b[2, 3])
    ones, twos = zip(*[send("row", r, b[r, 1], b[r, 2]) for r in (1, 2)])
    far_across = summed(b[3, 2], far_across)
    three = summed(after(b[0, 3], far_across), left, right)
    near_across = summed(after(b[3, 0], three), near_across)
    (far_across,), (three,) = send("row", 3, far_across), send("feat", 1, three)
    two = summed(b[0, 2], *twos, far_across, three)
    (two,), (near_across,) = send("feat", 2, two), send("row", 3, near_across)
    (one,) = send("feat", 1, summed(after(b[0, 1], near_across), *ones))
    near = b[0, 0]
    for r in (1, 2):
        near = near + send("row", r, after(b[r, 0], ones[0]))[0]
    return near + near_across + one + two


def any_mesh(samples, own_rows):
    row_total = samples.shape[0] * lax.axis_size("row") * lax.axis_size("feat")
    width_root = math.sqrt(samples.shape[1])
    for sweep in range(ITERS):
        dirs = lax.all_gather(
            own_rows.astype(jnp.bfloat16), ("row", "feat"), axis=0, tiled=True
        )
        summed_proj = jnp.dot(samples, dirs, preferred_element_type=jnp.float32)
        squares = lax.psum(jnp.sum(summed_proj * summed_proj, axis=0), ("row", "feat"))
        scaling = lax.rsqrt(squares / row_total + epsilon)
        own_proj = (summed_proj * scaling).astype(jnp.bfloat16)
        partner_proj = xor_move(own_proj, "view", 1)
        residue = (own_proj.astype(jnp.float32) - partner_proj.astype(jnp.float32)).astype(
            jnp.bfloat16
        )
        share = lax.dot_general(
            samples, residue, (((0,), (0,)), ((), ())), preferred_element_type=jnp.float32
        )
        share = lax.psum_scatter(share, ("row", "feat"), scatter_dimension=0, tiled=True)
        own_rows = width_root * (own_rows * scaling - step_rate * (share / row_total))
    return (own_rows[None], own_proj[None])


def regroup(samples, depth):
    rows_here = samples.shape[0]
    feats = lax.axis_size("feat")
    count = sum(len(places) for places in ARRIVALS)

    def kernel(samples_ref, *refs):
        outs, done = refs[:-1], refs[-1]
        row_at, feat_at = lax.axis_index("row"), lax.axis_index("feat")
        copies = []
        for out, places in zip(outs, ARRIVALS):
            for i, (r, t) in enumerate(places):
                start = pl.multiple_of(((row_at ^ r) * feats + (feat_at ^ t)) * depth, depth)
                copies.append(
                    pltpu.make_async_copy(
                        samples_ref.at[:, pl.ds(start, depth)],
                        out.at[:, pl.ds(i * depth, depth)],
                        done.at[len(copies)],
                    )
                )
                copies[-1].start()
        for copy in copies:
            copy.wait()

    return pl.pallas_call(
        kernel,
        out_shape=[
            jax.ShapeDtypeStruct((rows_here, len(places) * depth), samples.dtype)
            for places in ARRIVALS
        ],
        in_specs=[pl.BlockSpec(memory_space=pltpu.HBM)],
        out_specs=[pl.BlockSpec(memory_space=pl.ANY) for places in ARRIVALS],
        scratch_shapes=[pltpu.SemaphoreType.DMA((count,))],
        compiler_params=pltpu.CompilerParams(vmem_limit_bytes=1 << 20),
        cost_estimate=pl.CostEstimate(
            flops=0, bytes_accessed=2 * samples.size * 2, transcendentals=0
        ),
        name="regroup",
    )(samples)


def on_device(views, weights):
    samples = views[0]
    own_rows = weights[0]
    rows_here, width = samples.shape
    depth, pairs = own_rows.shape
    rows, feats = lax.axis_size("row"), lax.axis_size("feat")
    if (rows, feats) != (4, 4) or depth % 128:
        return any_mesh(samples, own_rows)
    row_total = rows_here * rows * feats
    width_root = math.sqrt(width)
    groups = regroup(samples, depth)
    for sweep in range(ITERS):
        dirs = gather(own_rows.astype(jnp.bfloat16))
        summed_proj = 0.0
        for g, places in enumerate(ARRIVALS):
            blocks = lax.optimization_barrier([dirs[p] for p in places])
            part = jnp.dot(
                groups[g], join(*blocks), preferred_element_type=jnp.float32
            )
            summed_proj = lax.optimization_barrier(summed_proj + part) if g < 2 else summed_proj + part
        kept_proj = lax.optimization_barrier(summed_proj.astype(jnp.bfloat16))
        partner_proj = xor_move(kept_proj, "view", 1).astype(jnp.float32)
        squares = jnp.sum(summed_proj * summed_proj, axis=0)
        scaling = lax.rsqrt(total(squares) / row_total + epsilon)
        partner_scaling = xor_move(scaling, "view", 1)
        own_proj = (kept_proj.astype(jnp.float32) * scaling).astype(jnp.bfloat16)
        partner_proj = (partner_proj * partner_scaling).astype(jnp.bfloat16)
        residue = (own_proj.astype(jnp.float32) - partner_proj.astype(jnp.float32)).astype(
            jnp.bfloat16
        )
        shares = {}
        for g in (2, 1, 0):
            share = lax.dot_general(
                groups[g], residue, (((0,), (0,)), ((), ())), preferred_element_type=jnp.float32
            )
            for i, place in enumerate(ARRIVALS[g]):
                shares[place] = share[i * depth : (i + 1) * depth]
        if sweep == ITERS - 1:
            kept_proj, shown_scaling = lax.optimization_barrier((kept_proj, scaling))
            own_proj = (kept_proj.astype(jnp.float32) * shown_scaling).astype(jnp.bfloat16)
        grad = scatter(shares) / row_total
        own_rows = width_root * (own_rows * scaling - step_rate * grad)
    return (own_rows[None], own_proj[None])


def solution(mesh):
    in_specs = (P("view", ("row", "feat"), None), P("view", ("row", "feat"), None))
    out_specs = (P("view", ("row", "feat"), None), P("view", ("row", "feat"), None))
    return jax.shard_map(
        on_device, mesh=mesh, in_specs=in_specs, out_specs=out_specs, check_vma=False
    )
```

```python
import math

import jax
import jax.numpy as jnp
from jax import lax
from jax.experimental import pallas as pl
from jax.experimental.pallas import tpu as pltpu
from jax.sharding import PartitionSpec as P

ITERS = 2


epsilon = 1e-06
step_rate = 0.5


def xor_move(block, axis, mask):
    count = lax.axis_size(axis)
    return lax.ppermute(block, axis, [(i, i ^ mask) for i in range(count)])


def after(value, *others):
    return lax.optimization_barrier((value,) + others)[0]


def total(values):
    for axis in ("row", "feat"):
        own = values
        for mask in reversed(range(1, lax.axis_size(axis))):
            values = lax.optimization_barrier(values + xor_move(own, axis, mask))
    return values


def join(*blocks):
    return jnp.concatenate(blocks, axis=0)


def split(pair):
    deep = pair.shape[0] // 2
    return pair[:deep], pair[deep:]


ARRIVALS = (
    ((0, 0), (1, 0), (2, 0), (3, 0), (0, 1), (0, 2)),
    ((0, 3), (3, 2), (1, 1), (1, 2), (2, 1), (2, 2)),
    ((3, 1), (3, 3), (1, 3), (2, 3)),
)


def gather(own):
    b = {(0, 0): own}
    b[0, 2] = xor_move(own, "feat", 2)
    b[0, 1] = xor_move(own, "feat", 1)
    for r in (3, 1, 2):
        b[r, 0] = xor_move(own, "row", r)
    b[3, 2] = xor_move(b[0, 2], "row", 3)
    b[0, 3] = xor_move(b[0, 2], "feat", 1)
    for r in (1, 2):
        pair = join(after(b[0, 1], b[0, 2]), b[0, 2])
        b[r, 1], b[r, 2] = split(xor_move(pair, "row", r))
    b[3, 1], b[3, 3] = split(xor_move(join(b[3, 0], b[3, 2]), "feat", 1))
    for r in (1, 2):
        b[r, 3] = xor_move(b[0, 3], "row", r)
    return b


def scatter(b):
    def send(axis, mask, *blocks):
        half = [block.astype(jnp.bfloat16) for block in blocks]
        got = xor_move(half[0] if len(half) == 1 else join(*half), axis, mask)
        return [part.astype(jnp.float32) for part in (split(got) if len(half) > 1 else [got])]

    def summed(first, *others):
        return lax.optimization_barrier(sum(others, first).astype(jnp.bfloat16))

    near_across, far_across = send("feat", 1, b[3, 1], b[3, 3])
    (left,), (right,) = send("row", 1, b[1, 3]), send("row", 2, b[2, 3])
    ones, twos = zip(*[send("row", r, b[r, 1], b[r, 2]) for r in (1, 2)])
    far_across = summed(b[3, 2], far_across)
    three = summed(after(b[0, 3], far_across), left, right)
    near_across = summed(after(b[3, 0], three), near_across)
    (far_across,), (three,) = send("row", 3, far_across), send("feat", 1, three)
    two = summed(b[0, 2], *twos, far_across, three)
    one = summed(after(b[0, 1], two), *ones)
    (two,), (near_across,), (one,) = (
        send("feat", 2, two),
        send("row", 3, near_across),
        send("feat", 1, one),
    )
    near = b[0, 0] + send("row", 1, b[1, 0])[0] + send("row", 2, b[2, 0])[0]
    return lax.optimization_barrier(near + two) + near_across + one


def any_mesh(samples, own_rows):
    row_total = samples.shape[0] * lax.axis_size("row") * lax.axis_size("feat")
    width_root = math.sqrt(samples.shape[1])
    for sweep in range(ITERS):
        dirs = lax.all_gather(
            own_rows.astype(jnp.bfloat16), ("row", "feat"), axis=0, tiled=True
        )
        summed_proj = jnp.dot(samples, dirs, preferred_element_type=jnp.float32)
        squares = lax.psum(jnp.sum(summed_proj * summed_proj, axis=0), ("row", "feat"))
        scaling = lax.rsqrt(squares / row_total + epsilon)
        own_proj = (summed_proj * scaling).astype(jnp.bfloat16)
        partner_proj = xor_move(own_proj, "view", 1)
        residue = (own_proj.astype(jnp.float32) - partner_proj.astype(jnp.float32)).astype(
            jnp.bfloat16
        )
        share = lax.dot_general(
            samples, residue, (((0,), (0,)), ((), ())), preferred_element_type=jnp.float32
        )
        share = lax.psum_scatter(share, ("row", "feat"), scatter_dimension=0, tiled=True)
        own_rows = width_root * (own_rows * scaling - step_rate * (share / row_total))
    return (own_rows[None], own_proj[None])


def regroup(samples, depth):
    rows_here = samples.shape[0]
    feats = lax.axis_size("feat")
    count = sum(len(places) for places in ARRIVALS)

    def kernel(samples_ref, *refs):
        outs, done = refs[:-1], refs[-1]
        row_at, feat_at = lax.axis_index("row"), lax.axis_index("feat")
        copies = []
        for out, places in zip(outs, ARRIVALS):
            for i, (r, t) in enumerate(places):
                start = pl.multiple_of(((row_at ^ r) * feats + (feat_at ^ t)) * depth, depth)
                copies.append(
                    pltpu.make_async_copy(
                        samples_ref.at[:, pl.ds(start, depth)],
                        out.at[:, pl.ds(i * depth, depth)],
                        done.at[len(copies)],
                    )
                )
                copies[-1].start()
        for copy in copies:
            copy.wait()

    return pl.pallas_call(
        kernel,
        out_shape=[
            jax.ShapeDtypeStruct((rows_here, len(places) * depth), samples.dtype)
            for places in ARRIVALS
        ],
        in_specs=[pl.BlockSpec(memory_space=pl.ANY)],
        out_specs=[pl.BlockSpec(memory_space=pl.ANY) for places in ARRIVALS],
        scratch_shapes=[pltpu.SemaphoreType.DMA((count,))],
        compiler_params=pltpu.CompilerParams(vmem_limit_bytes=44 << 20),
        cost_estimate=pl.CostEstimate(
            flops=0, bytes_accessed=2 * samples.size * 2, transcendentals=0
        ),
        name="regroup",
    )(samples)


def on_device(views, weights):
    samples = views[0]
    own_rows = weights[0]
    rows_here, width = samples.shape
    depth, pairs = own_rows.shape
    rows, feats = lax.axis_size("row"), lax.axis_size("feat")
    if (rows, feats) != (4, 4) or depth % 128:
        return any_mesh(samples, own_rows)
    row_total = rows_here * rows * feats
    width_root = math.sqrt(width)
    groups = regroup(samples, depth)
    for sweep in range(ITERS):
        dirs = gather(own_rows.astype(jnp.bfloat16))
        summed_proj = 0.0
        for g, places in enumerate(ARRIVALS):
            blocks = [dirs[p] for p in places]
            blocks = lax.optimization_barrier(blocks + [dirs[3, 2]])[: len(places)]
            part = jnp.dot(
                groups[g], join(*blocks), preferred_element_type=jnp.float32
            )
            summed_proj = lax.optimization_barrier(summed_proj + part) if g < 2 else summed_proj + part
        kept_proj = lax.optimization_barrier(summed_proj.astype(jnp.bfloat16))
        partner_proj = xor_move(kept_proj, "view", 1).astype(jnp.float32)
        squares = jnp.sum(summed_proj * summed_proj, axis=0)
        scaling = lax.rsqrt(total(squares) / row_total + epsilon)
        partner_scaling = xor_move(scaling, "view", 1)
        own_proj = (kept_proj.astype(jnp.float32) * scaling).astype(jnp.bfloat16)
        partner_proj = (partner_proj * partner_scaling).astype(jnp.bfloat16)
        residue = (own_proj.astype(jnp.float32) - partner_proj.astype(jnp.float32)).astype(
            jnp.bfloat16
        )
        shares = {}
        for g in (2, 1, 0):
            share = lax.dot_general(
                groups[g], residue, (((0,), (0,)), ((), ())), preferred_element_type=jnp.float32
            )
            for i, place in enumerate(ARRIVALS[g]):
                shares[place] = share[i * depth : (i + 1) * depth]
        if sweep == ITERS - 1:
            kept_proj, shown_scaling = lax.optimization_barrier((kept_proj, scaling))
            own_proj = (kept_proj.astype(jnp.float32) * shown_scaling).astype(jnp.bfloat16)
        grad = scatter(shares) / row_total
        own_rows = width_root * (own_rows * scaling - step_rate * grad)
    return (own_rows[None], own_proj[None])


def solution(mesh):
    in_specs = (P("view", ("row", "feat"), None), P("view", ("row", "feat"), None))
    out_specs = (P("view", ("row", "feat"), None), P("view", ("row", "feat"), None))
    return jax.shard_map(
        on_device, mesh=mesh, in_specs=in_specs, out_specs=out_specs, check_vma=False
    )
```

```python
import math

import jax
import jax.numpy as jnp
from jax import lax
from jax.experimental import pallas as pl
from jax.experimental.pallas import tpu as pltpu
from jax.sharding import PartitionSpec as P

ITERS = 2


epsilon = 1e-06
step_rate = 0.5


def xor_move(block, axis, mask):
    count = lax.axis_size(axis)
    return lax.ppermute(block, axis, [(i, i ^ mask) for i in range(count)])


def after(value, *others):
    return lax.optimization_barrier((value,) + others)[0]


def total(values):
    for axis in ("row", "feat"):
        own = values
        for mask in reversed(range(1, lax.axis_size(axis))):
            values = lax.optimization_barrier(values + xor_move(own, axis, mask))
    return values


def join(*blocks):
    return jnp.concatenate(blocks, axis=0)


def split(pair):
    deep = pair.shape[0] // 2
    return pair[:deep], pair[deep:]


ARRIVALS = (
    ((0, 0), (1, 0), (2, 0), (3, 0), (0, 1), (0, 2)),
    ((0, 3), (3, 2), (1, 1), (1, 2), (2, 1), (2, 2)),
    ((3, 1), (3, 3), (1, 3), (2, 3)),
)


def gather(own):
    b = {(0, 0): own}
    b[0, 2] = xor_move(own, "feat", 2)
    b[0, 1] = xor_move(own, "feat", 1)
    for r in (3, 1, 2):
        b[r, 0] = xor_move(own, "row", r)
    b[3, 2] = xor_move(b[0, 2], "row", 3)
    b[0, 3] = xor_move(b[0, 2], "feat", 1)
    for r in (1, 2):
        pair = join(after(b[0, 1], b[0, 2]), b[0, 2])
        b[r, 1], b[r, 2] = split(xor_move(pair, "row", r))
    b[3, 1], b[3, 3] = split(xor_move(join(b[3, 0], b[3, 2]), "feat", 1))
    for r in (1, 2):
        b[r, 3] = xor_move(b[0, 3], "row", r)
    return b


def scatter(b):
    def send(axis, mask, *blocks):
        half = [block.astype(jnp.bfloat16) for block in blocks]
        got = xor_move(half[0] if len(half) == 1 else join(*half), axis, mask)
        return [part.astype(jnp.float32) for part in (split(got) if len(half) > 1 else [got])]

    def summed(first, *others):
        return lax.optimization_barrier(sum(others, first).astype(jnp.bfloat16))

    near_across, far_across = send("feat", 1, b[3, 1], b[3, 3])
    (left,), (right,) = send("row", 1, b[1, 3]), send("row", 2, b[2, 3])
    ones, twos = zip(*[send("row", r, b[r, 1], b[r, 2]) for r in (1, 2)])
    far_across = summed(b[3, 2], far_across)
    three = summed(after(b[0, 3], far_across), left, right)
    near_across = summed(after(b[3, 0], three), near_across)
    (far_across,), (three,) = send("row", 3, far_across), send("feat", 1, three)
    two = summed(b[0, 2], *twos, far_across, three)
    one = summed(after(b[0, 1], two), *ones)
    (two,), (near_across,), (one,) = (
        send("feat", 2, two),
        send("row", 3, near_across),
        send("feat", 1, one),
    )
    near = b[0, 0] + send("row", 1, b[1, 0])[0] + send("row", 2, b[2, 0])[0]
    near = lax.optimization_barrier(near + near_across)
    return lax.optimization_barrier(near + two) + one


def any_mesh(samples, own_rows):
    row_total = samples.shape[0] * lax.axis_size("row") * lax.axis_size("feat")
    width_root = math.sqrt(samples.shape[1])
    for sweep in range(ITERS):
        dirs = lax.all_gather(
            own_rows.astype(jnp.bfloat16), ("row", "feat"), axis=0, tiled=True
        )
        summed_proj = jnp.dot(samples, dirs, preferred_element_type=jnp.float32)
        squares = lax.psum(jnp.sum(summed_proj * summed_proj, axis=0), ("row", "feat"))
        scaling = lax.rsqrt(squares / row_total + epsilon)
        own_proj = (summed_proj * scaling).astype(jnp.bfloat16)
        partner_proj = xor_move(own_proj, "view", 1)
        residue = (own_proj.astype(jnp.float32) - partner_proj.astype(jnp.float32)).astype(
            jnp.bfloat16
        )
        share = lax.dot_general(
            samples, residue, (((0,), (0,)), ((), ())), preferred_element_type=jnp.float32
        )
        share = lax.psum_scatter(share, ("row", "feat"), scatter_dimension=0, tiled=True)
        own_rows = width_root * (own_rows * scaling - step_rate * (share / row_total))
    return (own_rows[None], own_proj[None])


def regroup(samples, depth):
    rows_here = samples.shape[0]
    feats = lax.axis_size("feat")
    count = sum(len(places) for places in ARRIVALS)

    def kernel(samples_ref, *refs):
        outs, done = refs[:-1], refs[-1]
        row_at, feat_at = lax.axis_index("row"), lax.axis_index("feat")
        copies = []
        for out, places in zip(outs, ARRIVALS):
            for i, (r, t) in enumerate(places):
                start = pl.multiple_of(((row_at ^ r) * feats + (feat_at ^ t)) * depth, depth)
                copies.append(
                    pltpu.make_async_copy(
                        samples_ref.at[:, pl.ds(start, depth)],
                        out.at[:, pl.ds(i * depth, depth)],
                        done.at[len(copies)],
                    )
                )
                copies[-1].start()
        for copy in copies:
            copy.wait()

    return pl.pallas_call(
        kernel,
        out_shape=[
            jax.ShapeDtypeStruct((rows_here, len(places) * depth), samples.dtype)
            for places in ARRIVALS
        ],
        in_specs=[pl.BlockSpec(memory_space=pl.ANY)],
        out_specs=[pl.BlockSpec(memory_space=pl.ANY) for places in ARRIVALS],
        scratch_shapes=[pltpu.SemaphoreType.DMA((count,))],
        compiler_params=pltpu.CompilerParams(vmem_limit_bytes=42 << 20),
        cost_estimate=pl.CostEstimate(
            flops=0, bytes_accessed=2 * samples.size * 2, transcendentals=0
        ),
        name="regroup",
    )(samples)


def on_device(views, weights):
    samples = views[0]
    own_rows = weights[0]
    rows_here, width = samples.shape
    depth, pairs = own_rows.shape
    rows, feats = lax.axis_size("row"), lax.axis_size("feat")
    if (rows, feats) != (4, 4) or depth % 128:
        return any_mesh(samples, own_rows)
    row_total = rows_here * rows * feats
    width_root = math.sqrt(width)
    groups = regroup(samples, depth)
    for sweep in range(ITERS):
        dirs = gather(own_rows.astype(jnp.bfloat16))
        summed_proj = 0.0
        for g, places in enumerate(ARRIVALS):
            blocks = [dirs[p] for p in places]
            blocks = lax.optimization_barrier(blocks + [dirs[3, 2], dirs[0, 3]])[: len(places)]
            part = jnp.dot(
                groups[g], join(*blocks), preferred_element_type=jnp.float32
            )
            summed_proj = lax.optimization_barrier(summed_proj + part) if g < 2 else summed_proj + part
        kept_proj = lax.optimization_barrier(summed_proj.astype(jnp.bfloat16))
        partner_proj = xor_move(kept_proj, "view", 1).astype(jnp.float32)
        squares = jnp.sum(summed_proj * summed_proj, axis=0)
        scaling = lax.rsqrt(total(squares) / row_total + epsilon)
        partner_scaling = xor_move(scaling, "view", 1)
        own_proj = (kept_proj.astype(jnp.float32) * scaling).astype(jnp.bfloat16)
        partner_proj = (partner_proj * partner_scaling).astype(jnp.bfloat16)
        residue = (own_proj.astype(jnp.float32) - partner_proj.astype(jnp.float32)).astype(
            jnp.bfloat16
        )
        shares = {}
        for g in (2, 1, 0):
            share = lax.dot_general(
                groups[g], residue, (((0,), (0,)), ((), ())), preferred_element_type=jnp.float32
            )
            for i, place in enumerate(ARRIVALS[g]):
                shares[place] = share[i * depth : (i + 1) * depth]
        if sweep == ITERS - 1:
            kept_proj, shown_scaling = lax.optimization_barrier((kept_proj, scaling))
            own_proj = (kept_proj.astype(jnp.float32) * shown_scaling).astype(jnp.bfloat16)
        grad = scatter(shares) / row_total
        own_rows = width_root * (own_rows * scaling - step_rate * grad)
    return (own_rows[None], own_proj[None])


def solution(mesh):
    in_specs = (P("view", ("row", "feat"), None), P("view", ("row", "feat"), None))
    out_specs = (P("view", ("row", "feat"), None), P("view", ("row", "feat"), None))
    return jax.shard_map(
        on_device, mesh=mesh, in_specs=in_specs, out_specs=out_specs, check_vma=False
    )
```

```python
import math

import jax
import jax.numpy as jnp
from jax import lax
from jax.experimental import pallas as pl
from jax.experimental.pallas import tpu as pltpu
from jax.sharding import PartitionSpec as P

ITERS = 2


epsilon = 1e-06
step_rate = 0.5


def xor_move(block, axis, mask):
    count = lax.axis_size(axis)
    return lax.ppermute(block, axis, [(i, i ^ mask) for i in range(count)])


def after(value, *others):
    return lax.optimization_barrier((value,) + others)[0]


def total(values):
    for axis in ("row", "feat"):
        own = values
        for mask in reversed(range(1, lax.axis_size(axis))):
            values = lax.optimization_barrier(values + xor_move(own, axis, mask))
    return values


def join(*blocks):
    return jnp.concatenate(blocks, axis=0)


def split(pair):
    deep = pair.shape[0] // 2
    return pair[:deep], pair[deep:]


ARRIVALS = (
    ((0, 0), (1, 0), (2, 0), (3, 0), (0, 1), (0, 2)),
    ((0, 3), (3, 2), (1, 1), (1, 2), (2, 1), (2, 2)),
    ((3, 1), (3, 3), (1, 3), (2, 3)),
)


def gather(own):
    b = {(0, 0): own}
    b[0, 2] = xor_move(own, "feat", 2)
    b[0, 1] = xor_move(own, "feat", 1)
    for r in (3, 1, 2):
        b[r, 0] = xor_move(own, "row", r)
    b[3, 2] = xor_move(b[0, 2], "row", 3)
    b[0, 3] = xor_move(b[0, 2], "feat", 1)
    for r in (1, 2):
        pair = join(after(b[0, 1], b[0, 2]), b[0, 2])
        b[r, 1], b[r, 2] = split(xor_move(pair, "row", r))
    b[3, 1], b[3, 3] = split(xor_move(join(b[3, 0], b[3, 2]), "feat", 1))
    for r in (1, 2):
        b[r, 3] = xor_move(b[0, 3], "row", r)
    return b


def scatter(b):
    def send(axis, mask, *blocks):
        half = [block.astype(jnp.bfloat16) for block in blocks]
        got = xor_move(half[0] if len(half) == 1 else join(*half), axis, mask)
        return [part.astype(jnp.float32) for part in (split(got) if len(half) > 1 else [got])]

    def summed(first, *others):
        return lax.optimization_barrier(sum(others, first).astype(jnp.bfloat16))

    (far_across,), (near_across,) = send("feat", 1, b[3, 3]), send("feat", 1, b[3, 1])
    (left,), (right,) = send("row", 1, b[1, 3]), send("row", 2, b[2, 3])
    ones, twos = zip(*[send("row", r, b[r, 1], b[r, 2]) for r in (1, 2)])
    far_across = summed(b[3, 2], far_across)
    three = summed(after(b[0, 3], far_across), left, right)
    near_across = summed(after(b[3, 0], three), near_across)
    (far_across,), (three,) = send("row", 3, far_across), send("feat", 1, three)
    two = summed(b[0, 2], *twos, far_across, three)
    one = summed(after(b[0, 1], two), *ones)
    (two,), (near_across,), (one,) = (
        send("feat", 2, two),
        send("row", 3, near_across),
        send("feat", 1, one),
    )
    near = b[0, 0] + send("row", 1, b[1, 0])[0] + send("row", 2, b[2, 0])[0]
    return lax.optimization_barrier(near + two) + near_across + one


def any_mesh(samples, own_rows):
    row_total = samples.shape[0] * lax.axis_size("row") * lax.axis_size("feat")
    width_root = math.sqrt(samples.shape[1])
    for sweep in range(ITERS):
        dirs = lax.all_gather(
            own_rows.astype(jnp.bfloat16), ("row", "feat"), axis=0, tiled=True
        )
        summed_proj = jnp.dot(samples, dirs, preferred_element_type=jnp.float32)
        squares = lax.psum(jnp.sum(summed_proj * summed_proj, axis=0), ("row", "feat"))
        scaling = lax.rsqrt(squares / row_total + epsilon)
        own_proj = (summed_proj * scaling).astype(jnp.bfloat16)
        partner_proj = xor_move(own_proj, "view", 1)
        residue = (own_proj.astype(jnp.float32) - partner_proj.astype(jnp.float32)).astype(
            jnp.bfloat16
        )
        share = lax.dot_general(
            samples, residue, (((0,), (0,)), ((), ())), preferred_element_type=jnp.float32
        )
        share = lax.psum_scatter(share, ("row", "feat"), scatter_dimension=0, tiled=True)
        own_rows = width_root * (own_rows * scaling - step_rate * (share / row_total))
    return (own_rows[None], own_proj[None])


def regroup(samples, depth):
    rows_here = samples.shape[0]
    feats = lax.axis_size("feat")
    count = sum(len(places) for places in ARRIVALS)

    def kernel(samples_ref, *refs):
        outs, done = refs[:-1], refs[-1]
        row_at, feat_at = lax.axis_index("row"), lax.axis_index("feat")
        copies = []
        for out, places in zip(outs, ARRIVALS):
            for i, (r, t) in enumerate(places):
                start = pl.multiple_of(((row_at ^ r) * feats + (feat_at ^ t)) * depth, depth)
                copies.append(
                    pltpu.make_async_copy(
                        samples_ref.at[:, pl.ds(start, depth)],
                        out.at[:, pl.ds(i * depth, depth)],
                        done.at[len(copies)],
                    )
                )
                copies[-1].start()
        for copy in copies:
            copy.wait()

    return pl.pallas_call(
        kernel,
        out_shape=[
            jax.ShapeDtypeStruct((rows_here, len(places) * depth), samples.dtype)
            for places in ARRIVALS
        ],
        in_specs=[pl.BlockSpec(memory_space=pl.ANY)],
        out_specs=[pl.BlockSpec(memory_space=pl.ANY) for places in ARRIVALS],
        scratch_shapes=[pltpu.SemaphoreType.DMA((count,))],
        compiler_params=pltpu.CompilerParams(vmem_limit_bytes=1 << 20),
        cost_estimate=pl.CostEstimate(
            flops=0, bytes_accessed=2 * samples.size * 2, transcendentals=0
        ),
        name="regroup",
    )(samples)


def on_device(views, weights):
    samples = views[0]
    own_rows = weights[0]
    rows_here, width = samples.shape
    depth, pairs = own_rows.shape
    rows, feats = lax.axis_size("row"), lax.axis_size("feat")
    if (rows, feats) != (4, 4) or depth % 128:
        return any_mesh(samples, own_rows)
    row_total = rows_here * rows * feats
    width_root = math.sqrt(width)
    groups = regroup(samples, depth)
    for sweep in range(ITERS):
        dirs = gather(own_rows.astype(jnp.bfloat16))
        summed_proj = 0.0
        for g, places in enumerate(ARRIVALS):
            blocks = [dirs[p] for p in places]
            blocks = lax.optimization_barrier(blocks + [dirs[0, 3]])[: len(places)]
            part = jnp.dot(
                groups[g], join(*blocks), preferred_element_type=jnp.float32
            )
            summed_proj = lax.optimization_barrier(summed_proj + part) if g < 2 else summed_proj + part
        kept_proj = lax.optimization_barrier(summed_proj.astype(jnp.bfloat16))
        partner_proj = xor_move(kept_proj, "view", 1).astype(jnp.float32)
        squares = jnp.sum(summed_proj * summed_proj, axis=0)
        scaling = lax.rsqrt(total(squares) / row_total + epsilon)
        partner_scaling = xor_move(scaling, "view", 1)
        own_proj = (kept_proj.astype(jnp.float32) * scaling).astype(jnp.bfloat16)
        partner_proj = (partner_proj * partner_scaling).astype(jnp.bfloat16)
        residue = (own_proj.astype(jnp.float32) - partner_proj.astype(jnp.float32)).astype(
            jnp.bfloat16
        )
        shares = {}
        for g in (2, 1, 0):
            share = lax.dot_general(
                groups[g], residue, (((0,), (0,)), ((), ())), preferred_element_type=jnp.float32
            )
            for i, place in enumerate(ARRIVALS[g]):
                shares[place] = share[i * depth : (i + 1) * depth]
        if sweep == ITERS - 1:
            kept_proj, shown_scaling = lax.optimization_barrier((kept_proj, scaling))
            own_proj = (kept_proj.astype(jnp.float32) * shown_scaling).astype(jnp.bfloat16)
        grad = scatter(shares) / row_total
        own_rows = width_root * (own_rows * scaling - step_rate * grad)
    return (own_rows[None], own_proj[None])


def solution(mesh):
    in_specs = (P("view", ("row", "feat"), None), P("view", ("row", "feat"), None))
    out_specs = (P("view", ("row", "feat"), None), P("view", ("row", "feat"), None))
    return jax.shard_map(
        on_device, mesh=mesh, in_specs=in_specs, out_specs=out_specs, check_vma=False
    )
```

```python
import math

import jax
import jax.numpy as jnp
from jax import lax
from jax.experimental import pallas as pl
from jax.experimental.pallas import tpu as pltpu
from jax.sharding import PartitionSpec as P

ITERS = 2


epsilon = 1e-06
step_rate = 0.5


def xor_move(block, axis, mask):
    count = lax.axis_size(axis)
    return lax.ppermute(block, axis, [(i, i ^ mask) for i in range(count)])


def after(value, *others):
    return lax.optimization_barrier((value,) + others)[0]


def total(values):
    for axis in ("row", "feat"):
        own = values
        for mask in reversed(range(1, lax.axis_size(axis))):
            values = lax.optimization_barrier(values + xor_move(own, axis, mask))
    return values


def join(*blocks):
    return jnp.concatenate(blocks, axis=0)


def split(pair):
    deep = pair.shape[0] // 2
    return pair[:deep], pair[deep:]


ARRIVALS = (
    ((0, 0), (1, 0), (2, 0), (3, 0), (0, 1), (0, 2)),
    ((0, 3), (3, 2), (1, 1), (1, 2), (2, 1), (2, 2)),
    ((3, 1), (3, 3), (1, 3), (2, 3)),
)


def gather(own):
    b = {(0, 0): own}
    b[0, 2] = xor_move(own, "feat", 2)
    b[0, 1] = xor_move(own, "feat", 1)
    for r in (3, 1, 2):
        b[r, 0] = xor_move(own, "row", r)
    b[3, 2] = xor_move(b[0, 2], "row", 3)
    b[0, 3] = xor_move(b[0, 2], "feat", 1)
    for r in (1, 2):
        pair = join(after(b[0, 1], b[0, 2]), b[0, 2])
        b[r, 1], b[r, 2] = split(xor_move(pair, "row", r))
    b[3, 1], b[3, 3] = split(xor_move(join(b[3, 0], b[3, 2]), "feat", 1))
    for r in (1, 2):
        b[r, 3] = xor_move(b[0, 3], "row", r)
    return b


def scatter(b):
    def send(axis, mask, *blocks):
        half = [block.astype(jnp.bfloat16) for block in blocks]
        got = xor_move(half[0] if len(half) == 1 else join(*half), axis, mask)
        return [part.astype(jnp.float32) for part in (split(got) if len(half) > 1 else [got])]

    def summed(first, *others):
        return lax.optimization_barrier(sum(others, first).astype(jnp.bfloat16))

    near_across, far_across = send("feat", 1, b[3, 1], b[3, 3])
    (left,), (right,) = send("row", 1, b[1, 3]), send("row", 2, b[2, 3])
    ones, twos = zip(*[send("row", r, b[r, 1], b[r, 2]) for r in (1, 2)])
    far_across = summed(b[3, 2], far_across)
    three = summed(after(b[0, 3], far_across), left, right)
    near_across = summed(after(b[3, 0], three), near_across)
    (far_across,), (three,) = send("row", 3, far_across), send("feat", 1, three)
    two = summed(b[0, 2], *twos, far_across, three)
    one = summed(after(b[0, 1], two), *ones)
    (two,), (near_across,), (one,) = (
        send("feat", 2, two),
        send("row", 3, near_across),
        send("feat", 1, one),
    )
    near = b[0, 0] + send("row", 1, b[1, 0])[0] + send("row", 2, b[2, 0])[0]
    return lax.optimization_barrier(near + two) + near_across + one


def any_mesh(samples, own_rows):
    row_total = samples.shape[0] * lax.axis_size("row") * lax.axis_size("feat")
    width_root = math.sqrt(samples.shape[1])
    for sweep in range(ITERS):
        dirs = lax.all_gather(
            own_rows.astype(jnp.bfloat16), ("row", "feat"), axis=0, tiled=True
        )
        summed_proj = jnp.dot(samples, dirs, preferred_element_type=jnp.float32)
        squares = lax.psum(jnp.sum(summed_proj * summed_proj, axis=0), ("row", "feat"))
        scaling = lax.rsqrt(squares / row_total + epsilon)
        own_proj = (summed_proj * scaling).astype(jnp.bfloat16)
        partner_proj = xor_move(own_proj, "view", 1)
        residue = (own_proj.astype(jnp.float32) - partner_proj.astype(jnp.float32)).astype(
            jnp.bfloat16
        )
        share = lax.dot_general(
            samples, residue, (((0,), (0,)), ((), ())), preferred_element_type=jnp.float32
        )
        share = lax.psum_scatter(share, ("row", "feat"), scatter_dimension=0, tiled=True)
        own_rows = width_root * (own_rows * scaling - step_rate * (share / row_total))
    return (own_rows[None], own_proj[None])


def regroup(samples, depth):
    rows_here = samples.shape[0]
    feats = lax.axis_size("feat")
    count = sum(len(places) for places in ARRIVALS)

    def kernel(samples_ref, *refs):
        outs, done = refs[:-1], refs[-1]
        row_at, feat_at = lax.axis_index("row"), lax.axis_index("feat")
        copies = []
        for out, places in zip(outs, ARRIVALS):
            for i, (r, t) in enumerate(places):
                start = pl.multiple_of(((row_at ^ r) * feats + (feat_at ^ t)) * depth, depth)
                copies.append(
                    pltpu.make_async_copy(
                        samples_ref.at[:, pl.ds(start, depth)],
                        out.at[:, pl.ds(i * depth, depth)],
                        done.at[len(copies)],
                    )
                )
                copies[-1].start()
        for copy in copies:
            copy.wait()

    return pl.pallas_call(
        kernel,
        out_shape=[
            jax.ShapeDtypeStruct((rows_here, len(places) * depth), samples.dtype)
            for places in ARRIVALS
        ],
        in_specs=[pl.BlockSpec(memory_space=pl.ANY)],
        out_specs=[pl.BlockSpec(memory_space=pl.ANY) for places in ARRIVALS],
        scratch_shapes=[pltpu.SemaphoreType.DMA((count,))],
        compiler_params=pltpu.CompilerParams(vmem_limit_bytes=44 << 20),
        cost_estimate=pl.CostEstimate(
            flops=0, bytes_accessed=2 * samples.size * 2, transcendentals=0
        ),
        name="regroup",
    )(samples)


def scaled(proj, scaling):
    def kernel(proj_ref, scaling_ref, out_ref):
        columns = proj_ref[...].astype(jnp.float32)
        out_ref[...] = (columns.T * scaling_ref[...]).astype(out_ref.dtype)

    return pl.pallas_call(
        kernel,
        out_shape=jax.ShapeDtypeStruct(proj.shape, proj.dtype),
        in_specs=[pl.BlockSpec(memory_space=pltpu.VMEM)] * 2,
        out_specs=pl.BlockSpec(memory_space=pltpu.VMEM),
        compiler_params=pltpu.CompilerParams(vmem_limit_bytes=8 << 20),
        cost_estimate=pl.CostEstimate(
            flops=proj.size, bytes_accessed=4 * proj.size, transcendentals=0
        ),
        name="scaled",
    )(proj.T, scaling[None])


def on_device(views, weights):
    samples = views[0]
    own_rows = weights[0]
    rows_here, width = samples.shape
    depth, pairs = own_rows.shape
    rows, feats = lax.axis_size("row"), lax.axis_size("feat")
    if (rows, feats) != (4, 4) or depth % 128:
        return any_mesh(samples, own_rows)
    row_total = rows_here * rows * feats
    width_root = math.sqrt(width)
    groups = regroup(samples, depth)
    for sweep in range(ITERS):
        dirs = gather(own_rows.astype(jnp.bfloat16))
        summed_proj = 0.0
        for g, places in enumerate(ARRIVALS):
            blocks = [dirs[p] for p in places]
            blocks = lax.optimization_barrier(blocks + [dirs[0, 3]])[: len(places)]
            part = jnp.dot(
                groups[g], join(*blocks), preferred_element_type=jnp.float32
            )
            summed_proj = lax.optimization_barrier(summed_proj + part) if g < 2 else summed_proj + part
        kept_proj = lax.optimization_barrier(summed_proj.astype(jnp.bfloat16))
        partner_proj = xor_move(kept_proj, "view", 1).astype(jnp.float32)
        squares = jnp.sum(summed_proj * summed_proj, axis=0)
        scaling = lax.rsqrt(total(squares) / row_total + epsilon)
        partner_scaling = xor_move(scaling, "view", 1)
        own_proj = (kept_proj.astype(jnp.float32) * scaling).astype(jnp.bfloat16)
        partner_proj = (partner_proj * partner_scaling).astype(jnp.bfloat16)
        residue = (own_proj.astype(jnp.float32) - partner_proj.astype(jnp.float32)).astype(
            jnp.bfloat16
        )
        shares = {}
        for g in (2, 1, 0):
            share = lax.dot_general(
                groups[g], residue, (((0,), (0,)), ((), ())), preferred_element_type=jnp.float32
            )
            for i, place in enumerate(ARRIVALS[g]):
                shares[place] = share[i * depth : (i + 1) * depth]
        if sweep == ITERS - 1:
            shown = scaled(kept_proj, scaling)
        grad = scatter(shares) / row_total
        own_rows = width_root * (own_rows * scaling - step_rate * grad)
    return (own_rows[None], shown[None])


def solution(mesh):
    in_specs = (P("view", ("row", "feat"), None), P("view", ("row", "feat"), None))
    out_specs = (P("view", ("row", "feat"), None), P("view", ("row", "feat"), None))
    return jax.shard_map(
        on_device, mesh=mesh, in_specs=in_specs, out_specs=out_specs, check_vma=False
    )
```

```python
import math

import jax
import jax.numpy as jnp
from jax import lax
from jax.experimental import pallas as pl
from jax.experimental.pallas import tpu as pltpu
from jax.sharding import PartitionSpec as P

ITERS = 2


epsilon = 1e-06
step_rate = 0.5


def xor_move(block, axis, mask):
    count = lax.axis_size(axis)
    return lax.ppermute(block, axis, [(i, i ^ mask) for i in range(count)])


def after(value, *others):
    return lax.optimization_barrier((value,) + others)[0]


def total(values):
    for axis in ("row", "feat"):
        own = values
        for mask in reversed(range(1, lax.axis_size(axis))):
            values = lax.optimization_barrier(values + xor_move(own, axis, mask))
    return values


def join(*blocks):
    return jnp.concatenate(blocks, axis=0)


def split(pair):
    deep = pair.shape[0] // 2
    return pair[:deep], pair[deep:]


ARRIVALS = (
    ((0, 0), (1, 0), (2, 0), (3, 0), (0, 1), (0, 2)),
    ((0, 3), (3, 2), (1, 1), (1, 2), (2, 1), (2, 2)),
    ((3, 1), (3, 3), (1, 3), (2, 3)),
)


def gather(own):
    b = {(0, 0): own}
    b[0, 2] = xor_move(own, "feat", 2)
    b[0, 1] = xor_move(own, "feat", 1)
    for r in (3, 1, 2):
        b[r, 0] = xor_move(own, "row", r)
    b[3, 2] = xor_move(b[0, 2], "row", 3)
    b[0, 3] = xor_move(b[0, 2], "feat", 1)
    for r in (1, 2):
        pair = join(after(b[0, 1], b[0, 2]), b[0, 2])
        b[r, 1], b[r, 2] = split(xor_move(pair, "row", r))
    b[3, 1], b[3, 3] = split(xor_move(join(b[3, 0], b[3, 2]), "feat", 1))
    for r in (1, 2):
        b[r, 3] = xor_move(b[0, 3], "row", r)
    return b


def scatter(b):
    def send(axis, mask, *blocks):
        got = xor_move(blocks[0] if len(blocks) == 1 else join(*blocks), axis, mask)
        return [part.astype(jnp.float32) for part in (split(got) if len(blocks) > 1 else [got])]

    def summed(first, *others):
        sums = sum(others, first.astype(jnp.float32))
        return lax.optimization_barrier(sums.astype(jnp.bfloat16))

    near_across, far_across = send("feat", 1, b[3, 1], b[3, 3])
    (left,), (right,) = send("row", 1, b[1, 3]), send("row", 2, b[2, 3])
    ones, twos = zip(*[send("row", r, b[r, 1], b[r, 2]) for r in (1, 2)])
    far_across = summed(b[3, 2], far_across)
    three = summed(after(b[0, 3], far_across), left, right)
    near_across = summed(after(b[3, 0], three), near_across)
    (far_across,), (three,) = send("row", 3, far_across), send("feat", 1, three)
    two = summed(b[0, 2], *twos, far_across, three)
    one = summed(after(b[0, 1], two), *ones)
    (two,), (near_across,), (one,) = (
        send("feat", 2, two),
        send("row", 3, near_across),
        send("feat", 1, one),
    )
    near = b[0, 0].astype(jnp.float32) + send("row", 1, b[1, 0])[0] + send("row", 2, b[2, 0])[0]
    return lax.optimization_barrier(near + two) + near_across + one


def any_mesh(samples, own_rows):
    row_total = samples.shape[0] * lax.axis_size("row") * lax.axis_size("feat")
    width_root = math.sqrt(samples.shape[1])
    for sweep in range(ITERS):
        dirs = lax.all_gather(
            own_rows.astype(jnp.bfloat16), ("row", "feat"), axis=0, tiled=True
        )
        summed_proj = jnp.dot(samples, dirs, preferred_element_type=jnp.float32)
        squares = lax.psum(jnp.sum(summed_proj * summed_proj, axis=0), ("row", "feat"))
        scaling = lax.rsqrt(squares / row_total + epsilon)
        own_proj = (summed_proj * scaling).astype(jnp.bfloat16)
        partner_proj = xor_move(own_proj, "view", 1)
        residue = (own_proj.astype(jnp.float32) - partner_proj.astype(jnp.float32)).astype(
            jnp.bfloat16
        )
        share = lax.dot_general(
            samples, residue, (((0,), (0,)), ((), ())), preferred_element_type=jnp.float32
        )
        share = lax.psum_scatter(share, ("row", "feat"), scatter_dimension=0, tiled=True)
        own_rows = width_root * (own_rows * scaling - step_rate * (share / row_total))
    return (own_rows[None], own_proj[None])


def regroup(samples, depth):
    rows_here = samples.shape[0]
    feats = lax.axis_size("feat")
    count = sum(len(places) for places in ARRIVALS)

    def kernel(samples_ref, *refs):
        outs, done = refs[:-1], refs[-1]
        row_at, feat_at = lax.axis_index("row"), lax.axis_index("feat")
        copies = []
        for out, places in zip(outs, ARRIVALS):
            for i, (r, t) in enumerate(places):
                start = pl.multiple_of(((row_at ^ r) * feats + (feat_at ^ t)) * depth, depth)
                copies.append(
                    pltpu.make_async_copy(
                        samples_ref.at[:, pl.ds(start, depth)],
                        out.at[:, pl.ds(i * depth, depth)],
                        done.at[len(copies)],
                    )
                )
                copies[-1].start()
        for copy in copies:
            copy.wait()

    return pl.pallas_call(
        kernel,
        out_shape=[
            jax.ShapeDtypeStruct((rows_here, len(places) * depth), samples.dtype)
            for places in ARRIVALS
        ],
        in_specs=[pl.BlockSpec(memory_space=pl.ANY)],
        out_specs=[pl.BlockSpec(memory_space=pl.ANY) for places in ARRIVALS],
        scratch_shapes=[pltpu.SemaphoreType.DMA((count,))],
        compiler_params=pltpu.CompilerParams(vmem_limit_bytes=44 << 20),
        cost_estimate=pl.CostEstimate(
            flops=0, bytes_accessed=2 * samples.size * 2, transcendentals=0
        ),
        name="regroup",
    )(samples)


def scaled(proj, scaling):
    def kernel(proj_ref, scaling_ref, out_ref):
        columns = proj_ref[...].astype(jnp.float32)
        out_ref[...] = (columns.T * scaling_ref[...]).astype(out_ref.dtype)

    return pl.pallas_call(
        kernel,
        out_shape=jax.ShapeDtypeStruct(proj.shape, proj.dtype),
        in_specs=[pl.BlockSpec(memory_space=pltpu.VMEM)] * 2,
        out_specs=pl.BlockSpec(memory_space=pltpu.VMEM),
        compiler_params=pltpu.CompilerParams(vmem_limit_bytes=8 << 20),
        cost_estimate=pl.CostEstimate(
            flops=proj.size, bytes_accessed=4 * proj.size, transcendentals=0
        ),
        name="scaled",
    )(proj.T, scaling[None])


def on_device(views, weights):
    samples = views[0]
    own_rows = weights[0]
    rows_here, width = samples.shape
    depth, pairs = own_rows.shape
    rows, feats = lax.axis_size("row"), lax.axis_size("feat")
    if (rows, feats) != (4, 4) or depth % 128:
        return any_mesh(samples, own_rows)
    row_total = rows_here * rows * feats
    width_root = math.sqrt(width)
    for sweep in range(ITERS):
        dirs = gather(own_rows.astype(jnp.bfloat16))
        if sweep == 0:
            groups = regroup(after(samples, dirs[1, 0]), depth)
        summed_proj = 0.0
        for g, places in enumerate(ARRIVALS):
            blocks = [dirs[p] for p in places]
            blocks = lax.optimization_barrier(blocks + [dirs[0, 3]])[: len(places)]
            part = jnp.dot(
                groups[g], join(*blocks), preferred_element_type=jnp.float32
            )
            summed_proj = lax.optimization_barrier(summed_proj + part) if g < 2 else summed_proj + part
        kept_proj = lax.optimization_barrier(summed_proj.astype(jnp.bfloat16))
        partner_proj = xor_move(kept_proj, "view", 1).astype(jnp.float32)
        squares = jnp.sum(summed_proj * summed_proj, axis=0)
        scaling = lax.rsqrt(total(squares) / row_total + epsilon)
        partner_scaling = xor_move(scaling, "view", 1)
        own_proj = (kept_proj.astype(jnp.float32) * scaling).astype(jnp.bfloat16)
        partner_proj = (partner_proj * partner_scaling).astype(jnp.bfloat16)
        residue = (own_proj.astype(jnp.float32) - partner_proj.astype(jnp.float32)).astype(
            jnp.bfloat16
        )
        shares = {}
        for g in (2, 1, 0):
            share = lax.dot_general(
                groups[g], residue, (((0,), (0,)), ((), ())), preferred_element_type=jnp.float32
            ).astype(jnp.bfloat16)
            for i, place in enumerate(ARRIVALS[g]):
                shares[place] = share[i * depth : (i + 1) * depth]
        if sweep == ITERS - 1:
            shown = scaled(kept_proj, scaling)
        grad = scatter(shares) / row_total
        own_rows = width_root * (own_rows * scaling - step_rate * grad)
    return (own_rows[None], shown[None])


def solution(mesh):
    in_specs = (P("view", ("row", "feat"), None), P("view", ("row", "feat"), None))
    out_specs = (P("view", ("row", "feat"), None), P("view", ("row", "feat"), None))
    return jax.shard_map(
        on_device, mesh=mesh, in_specs=in_specs, out_specs=out_specs, check_vma=False
    )
```

```python
import math

import jax
import jax.numpy as jnp
from jax import lax
from jax.experimental import pallas as pl
from jax.experimental.pallas import tpu as pltpu
from jax.sharding import PartitionSpec as P

ITERS = 2


epsilon = 1e-06
step_rate = 0.5


def xor_move(block, axis, mask):
    count = lax.axis_size(axis)
    return lax.ppermute(block, axis, [(i, i ^ mask) for i in range(count)])


def after(value, *others):
    return lax.optimization_barrier((value,) + others)[0]


def total(values):
    for axis in ("row", "feat"):
        own = values
        for mask in reversed(range(1, lax.axis_size(axis))):
            values = lax.optimization_barrier(values + xor_move(own, axis, mask))
    return values


def join(*blocks):
    return jnp.concatenate(blocks, axis=1)


def split(pair):
    deep = pair.shape[1] // 2
    return pair[:, :deep], pair[:, deep:]


ARRIVALS = (
    ((0, 0), (1, 0), (2, 0), (3, 0), (0, 1), (0, 2)),
    ((0, 3), (3, 2), (1, 1), (1, 2), (2, 1), (2, 2)),
    ((3, 1), (3, 3), (1, 3), (2, 3)),
)


def gather(own):
    b = {(0, 0): own}
    b[0, 2] = xor_move(own, "feat", 2)
    b[0, 1] = xor_move(own, "feat", 1)
    for r in (3, 1, 2):
        b[r, 0] = xor_move(own, "row", r)
    b[3, 2] = xor_move(b[0, 2], "row", 3)
    b[0, 3] = xor_move(b[0, 2], "feat", 1)
    for r in (1, 2):
        pair = join(after(b[0, 1], b[0, 2]), b[0, 2])
        b[r, 1], b[r, 2] = split(xor_move(pair, "row", r))
    b[3, 1], b[3, 3] = split(xor_move(join(b[3, 0], b[3, 2]), "feat", 1))
    for r in (1, 2):
        b[r, 3] = xor_move(b[0, 3], "row", r)
    return b


def scatter(b):
    def send(axis, mask, *blocks):
        half = [block.astype(jnp.bfloat16) for block in blocks]
        got = xor_move(half[0] if len(half) == 1 else join(*half), axis, mask)
        return [part.astype(jnp.float32) for part in (split(got) if len(half) > 1 else [got])]

    def summed(first, *others):
        return lax.optimization_barrier(sum(others, first).astype(jnp.bfloat16))

    near_across, far_across = send("feat", 1, b[3, 1], b[3, 3])
    (left,), (right,) = send("row", 1, b[1, 3]), send("row", 2, b[2, 3])
    ones, twos = zip(*[send("row", r, b[r, 1], b[r, 2]) for r in (1, 2)])
    far_across = summed(b[3, 2], far_across)
    three = summed(after(b[0, 3], far_across), left, right)
    near_across = summed(after(b[3, 0], three), near_across)
    (far_across,), (three,) = send("row", 3, far_across), send("feat", 1, three)
    two = summed(b[0, 2], *twos, far_across, three)
    one = summed(after(b[0, 1], two), *ones)
    (two,), (near_across,), (one,) = (
        send("feat", 2, two),
        send("row", 3, near_across),
        send("feat", 1, one),
    )
    near = b[0, 0] + send("row", 1, b[1, 0])[0] + send("row", 2, b[2, 0])[0]
    return lax.optimization_barrier(near + two) + near_across + one


def any_mesh(samples, own_rows):
    row_total = samples.shape[0] * lax.axis_size("row") * lax.axis_size("feat")
    width_root = math.sqrt(samples.shape[1])
    for sweep in range(ITERS):
        dirs = lax.all_gather(
            own_rows.astype(jnp.bfloat16), ("row", "feat"), axis=0, tiled=True
        )
        summed_proj = jnp.dot(samples, dirs, preferred_element_type=jnp.float32)
        squares = lax.psum(jnp.sum(summed_proj * summed_proj, axis=0), ("row", "feat"))
        scaling = lax.rsqrt(squares / row_total + epsilon)
        own_proj = (summed_proj * scaling).astype(jnp.bfloat16)
        partner_proj = xor_move(own_proj, "view", 1)
        residue = (own_proj.astype(jnp.float32) - partner_proj.astype(jnp.float32)).astype(
            jnp.bfloat16
        )
        share = lax.dot_general(
            samples, residue, (((0,), (0,)), ((), ())), preferred_element_type=jnp.float32
        )
        share = lax.psum_scatter(share, ("row", "feat"), scatter_dimension=0, tiled=True)
        own_rows = width_root * (own_rows * scaling - step_rate * (share / row_total))
    return (own_rows[None], own_proj[None])


def regroup(samples, depth):
    rows_here = samples.shape[0]
    feats = lax.axis_size("feat")
    count = sum(len(places) for places in ARRIVALS)

    def kernel(samples_ref, *refs):
        outs, done = refs[:-1], refs[-1]
        row_at, feat_at = lax.axis_index("row"), lax.axis_index("feat")
        copies = []
        for out, places in zip(outs, ARRIVALS):
            for i, (r, t) in enumerate(places):
                start = pl.multiple_of(((row_at ^ r) * feats + (feat_at ^ t)) * depth, depth)
                copies.append(
                    pltpu.make_async_copy(
                        samples_ref.at[:, pl.ds(start, depth)],
                        out.at[:, pl.ds(i * depth, depth)],
                        done.at[len(copies)],
                    )
                )
                copies[-1].start()
        for copy in copies:
            copy.wait()

    return pl.pallas_call(
        kernel,
        out_shape=[
            jax.ShapeDtypeStruct((rows_here, len(places) * depth), samples.dtype)
            for places in ARRIVALS
        ],
        in_specs=[pl.BlockSpec(memory_space=pl.ANY)],
        out_specs=[pl.BlockSpec(memory_space=pl.ANY) for places in ARRIVALS],
        scratch_shapes=[pltpu.SemaphoreType.DMA((count,))],
        compiler_params=pltpu.CompilerParams(vmem_limit_bytes=44 << 20),
        cost_estimate=pl.CostEstimate(
            flops=0, bytes_accessed=2 * samples.size * 2, transcendentals=0
        ),
        name="regroup",
    )(samples)


def scaled(proj, scaling):
    def kernel(proj_ref, scaling_ref, out_ref):
        columns = proj_ref[...].astype(jnp.float32).T
        out_ref[...] = (columns * scaling_ref[...]).astype(out_ref.dtype)

    return pl.pallas_call(
        kernel,
        out_shape=jax.ShapeDtypeStruct(proj.shape[::-1], proj.dtype),
        in_specs=[pl.BlockSpec(memory_space=pltpu.VMEM)] * 2,
        out_specs=pl.BlockSpec(memory_space=pltpu.VMEM),
        compiler_params=pltpu.CompilerParams(vmem_limit_bytes=8 << 20),
        cost_estimate=pl.CostEstimate(
            flops=proj.size, bytes_accessed=4 * proj.size, transcendentals=0
        ),
        name="scaled",
    )(proj, scaling[None])


def on_device(views, weights):
    samples = views[0]
    own_rows = weights[0]
    rows_here, width = samples.shape
    depth, pairs = own_rows.shape
    rows, feats = lax.axis_size("row"), lax.axis_size("feat")
    if (rows, feats) != (4, 4) or depth % 128:
        return any_mesh(samples, own_rows)
    row_total = rows_here * rows * feats
    width_root = math.sqrt(width)
    groups = regroup(samples, depth)
    dirs_t = own_rows.T
    for sweep in range(ITERS):
        dirs = gather(dirs_t.astype(jnp.bfloat16))
        summed_proj = 0.0
        for g, places in enumerate(ARRIVALS):
            blocks = [dirs[p] for p in places]
            blocks = lax.optimization_barrier(blocks + [dirs[0, 3]])[: len(places)]
            part = lax.dot_general(
                join(*blocks),
                groups[g],
                (((1,), (1,)), ((), ())),
                preferred_element_type=jnp.float32,
            )
            summed_proj = summed_proj + part
            if g < len(ARRIVALS) - 1:
                summed_proj = lax.optimization_barrier(summed_proj)
        kept_proj = lax.optimization_barrier(summed_proj.astype(jnp.bfloat16))
        partner_proj = xor_move(kept_proj, "view", 1).astype(jnp.float32)
        squares = jnp.sum(summed_proj * summed_proj, axis=1)
        scaling = lax.rsqrt(total(squares) / row_total + epsilon)
        partner_scaling = xor_move(scaling, "view", 1)
        own_proj = (kept_proj.astype(jnp.float32) * scaling[:, None]).astype(jnp.bfloat16)
        partner_proj = (partner_proj * partner_scaling[:, None]).astype(jnp.bfloat16)
        residue = (own_proj.astype(jnp.float32) - partner_proj.astype(jnp.float32)).astype(
            jnp.bfloat16
        )
        shares = {}
        for g in (2, 1, 0):
            share = lax.dot_general(
                residue, groups[g], (((1,), (0,)), ((), ())), preferred_element_type=jnp.float32
            )
            for i, place in enumerate(ARRIVALS[g]):
                shares[place] = share[:, i * depth : (i + 1) * depth]
        if sweep == ITERS - 1:
            shown = scaled(kept_proj, scaling)
        grad = scatter(shares) / row_total
        dirs_t = width_root * (dirs_t * scaling[:, None] - step_rate * grad)
    return (dirs_t.T[None], shown[None])


def solution(mesh):
    in_specs = (P("view", ("row", "feat"), None), P("view", ("row", "feat"), None))
    out_specs = (P("view", ("row", "feat"), None), P("view", ("row", "feat"), None))
    return jax.shard_map(
        on_device, mesh=mesh, in_specs=in_specs, out_specs=out_specs, check_vma=False
    )
```

```python
import math

import jax
import jax.numpy as jnp
from jax import lax
from jax.experimental import pallas as pl
from jax.experimental.pallas import tpu as pltpu
from jax.sharding import PartitionSpec as P

ITERS = 2


epsilon = 1e-06
step_rate = 0.5


def xor_move(block, axis, mask):
    count = lax.axis_size(axis)
    return lax.ppermute(block, axis, [(i, i ^ mask) for i in range(count)])


def after(value, *others):
    return lax.optimization_barrier((value,) + others)[0]


def total(values):
    for axis in ("row", "feat"):
        own = values
        for mask in reversed(range(1, lax.axis_size(axis))):
            values = lax.optimization_barrier(values + xor_move(own, axis, mask))
    return values


def join(*blocks):
    return jnp.concatenate(blocks, axis=1)


def split(pair):
    deep = pair.shape[1] // 2
    return pair[:, :deep], pair[:, deep:]


ARRIVALS = (
    ((0, 0), (1, 0), (2, 0), (3, 0), (0, 1), (0, 2)),
    ((0, 3), (3, 2), (1, 1), (1, 2), (2, 1), (2, 2)),
    ((3, 1), (3, 3), (1, 3), (2, 3)),
)


def gather(own):
    b = {(0, 0): own}
    b[0, 2] = xor_move(own, "feat", 2)
    b[0, 1] = xor_move(own, "feat", 1)
    for r in (3, 1, 2):
        b[r, 0] = xor_move(own, "row", r)
    b[3, 2] = xor_move(b[0, 2], "row", 3)
    b[0, 3] = xor_move(b[0, 2], "feat", 1)
    for r in (1, 2):
        pair = join(after(b[0, 1], b[0, 2]), b[0, 2])
        b[r, 1], b[r, 2] = split(xor_move(pair, "row", r))
    b[3, 1], b[3, 3] = split(xor_move(join(b[3, 0], b[3, 2]), "feat", 1))
    for r in (1, 2):
        b[r, 3] = xor_move(b[0, 3], "row", r)
    return b


def scatter(b):
    def send(axis, mask, *blocks):
        half = [block.astype(jnp.bfloat16) for block in blocks]
        got = xor_move(half[0] if len(half) == 1 else join(*half), axis, mask)
        return [part.astype(jnp.float32) for part in (split(got) if len(half) > 1 else [got])]

    def summed(first, *others):
        return lax.optimization_barrier(sum(others, first).astype(jnp.bfloat16))

    near_across, far_across = send("feat", 1, b[3, 1], b[3, 3])
    (left,), (right,) = send("row", 1, b[1, 3]), send("row", 2, b[2, 3])
    ones, twos = zip(*[send("row", r, b[r, 1], b[r, 2]) for r in (1, 2)])
    far_across = summed(b[3, 2], far_across)
    three = summed(after(b[0, 3], far_across), left, right)
    (far_across,), (three,) = send("row", 3, far_across), send("feat", 1, three)
    two = summed(b[0, 2], *twos, far_across, three)
    near_across = summed(after(b[3, 0], two), near_across)
    one = summed(after(b[0, 1], two), *ones)
    (two,), (near_across,), (one,) = (
        send("feat", 2, two),
        send("row", 3, near_across),
        send("feat", 1, one),
    )
    near = b[0, 0] + send("row", 1, b[1, 0])[0] + send("row", 2, b[2, 0])[0]
    return lax.optimization_barrier(near + two) + near_across + one


def any_mesh(samples, own_rows):
    row_total = samples.shape[0] * lax.axis_size("row") * lax.axis_size("feat")
    width_root = math.sqrt(samples.shape[1])
    for sweep in range(ITERS):
        dirs = lax.all_gather(
            own_rows.astype(jnp.bfloat16), ("row", "feat"), axis=0, tiled=True
        )
        summed_proj = jnp.dot(samples, dirs, preferred_element_type=jnp.float32)
        squares = lax.psum(jnp.sum(summed_proj * summed_proj, axis=0), ("row", "feat"))
        scaling = lax.rsqrt(squares / row_total + epsilon)
        own_proj = (summed_proj * scaling).astype(jnp.bfloat16)
        partner_proj = xor_move(own_proj, "view", 1)
        residue = (own_proj.astype(jnp.float32) - partner_proj.astype(jnp.float32)).astype(
            jnp.bfloat16
        )
        share = lax.dot_general(
            samples, residue, (((0,), (0,)), ((), ())), preferred_element_type=jnp.float32
        )
        share = lax.psum_scatter(share, ("row", "feat"), scatter_dimension=0, tiled=True)
        own_rows = width_root * (own_rows * scaling - step_rate * (share / row_total))
    return (own_rows[None], own_proj[None])


def regroup(samples, depth):
    rows_here = samples.shape[0]
    feats = lax.axis_size("feat")
    count = sum(len(places) for places in ARRIVALS)

    def kernel(samples_ref, *refs):
        outs, done = refs[:-1], refs[-1]
        row_at, feat_at = lax.axis_index("row"), lax.axis_index("feat")
        copies = []
        for out, places in zip(outs, ARRIVALS):
            for i, (r, t) in enumerate(places):
                start = pl.multiple_of(((row_at ^ r) * feats + (feat_at ^ t)) * depth, depth)
                copies.append(
                    pltpu.make_async_copy(
                        samples_ref.at[:, pl.ds(start, depth)],
                        out.at[:, pl.ds(i * depth, depth)],
                        done.at[len(copies)],
                    )
                )
                copies[-1].start()
        for copy in copies:
            copy.wait()

    return pl.pallas_call(
        kernel,
        out_shape=[
            jax.ShapeDtypeStruct((rows_here, len(places) * depth), samples.dtype)
            for places in ARRIVALS
        ],
        in_specs=[pl.BlockSpec(memory_space=pl.ANY)],
        out_specs=[pl.BlockSpec(memory_space=pl.ANY) for places in ARRIVALS],
        scratch_shapes=[pltpu.SemaphoreType.DMA((count,))],
        compiler_params=pltpu.CompilerParams(vmem_limit_bytes=44 << 20),
        cost_estimate=pl.CostEstimate(
            flops=0, bytes_accessed=2 * samples.size * 2, transcendentals=0
        ),
        name="regroup",
    )(samples)


def scaled(proj, scaling):
    def kernel(proj_ref, scaling_ref, out_ref):
        columns = proj_ref[...].astype(jnp.float32).T
        out_ref[...] = (columns * scaling_ref[...]).astype(out_ref.dtype)

    return pl.pallas_call(
        kernel,
        out_shape=jax.ShapeDtypeStruct(proj.shape[::-1], proj.dtype),
        in_specs=[pl.BlockSpec(memory_space=pltpu.VMEM)] * 2,
        out_specs=pl.BlockSpec(memory_space=pltpu.VMEM),
        compiler_params=pltpu.CompilerParams(vmem_limit_bytes=8 << 20),
        cost_estimate=pl.CostEstimate(
            flops=proj.size, bytes_accessed=4 * proj.size, transcendentals=0
        ),
        name="scaled",
    )(proj, scaling[None])


def on_device(views, weights):
    samples = views[0]
    own_rows = weights[0]
    rows_here, width = samples.shape
    depth, pairs = own_rows.shape
    rows, feats = lax.axis_size("row"), lax.axis_size("feat")
    if (rows, feats) != (4, 4) or depth % 128:
        return any_mesh(samples, own_rows)
    row_total = rows_here * rows * feats
    width_root = math.sqrt(width)
    groups = regroup(samples, depth)
    dirs_t = own_rows.T
    for sweep in range(ITERS):
        dirs = gather(dirs_t.astype(jnp.bfloat16))
        summed_proj = 0.0
        for g, places in enumerate(ARRIVALS):
            blocks = [dirs[p] for p in places]
            blocks = lax.optimization_barrier(blocks + [dirs[3, 2], dirs[0, 3]])[: len(places)]
            part = lax.dot_general(
                join(*blocks),
                groups[g],
                (((1,), (1,)), ((), ())),
                preferred_element_type=jnp.float32,
            )
            summed_proj = summed_proj + part
            if g < len(ARRIVALS) - 1:
                summed_proj = lax.optimization_barrier(summed_proj)
        kept_proj = lax.optimization_barrier(summed_proj.astype(jnp.bfloat16))
        partner_proj = xor_move(kept_proj, "view", 1).astype(jnp.float32)
        squares = jnp.sum(summed_proj * summed_proj, axis=1)
        scaling = lax.rsqrt(total(squares) / row_total + epsilon)
        partner_scaling = xor_move(scaling, "view", 1)
        own_proj = (kept_proj.astype(jnp.float32) * scaling[:, None]).astype(jnp.bfloat16)
        partner_proj = (partner_proj * partner_scaling[:, None]).astype(jnp.bfloat16)
        residue = (own_proj.astype(jnp.float32) - partner_proj.astype(jnp.float32)).astype(
            jnp.bfloat16
        )
        shares = {}
        for g in (2, 1, 0):
            share = lax.dot_general(
                residue, groups[g], (((1,), (0,)), ((), ())), preferred_element_type=jnp.float32
            )
            for i, place in enumerate(ARRIVALS[g]):
                shares[place] = share[:, i * depth : (i + 1) * depth]
        if sweep == ITERS - 1:
            shown = scaled(kept_proj, scaling)
        grad = scatter(shares) / row_total
        dirs_t = width_root * (dirs_t * scaling[:, None] - step_rate * grad)
    return (dirs_t.T[None], shown[None])


def solution(mesh):
    in_specs = (P("view", ("row", "feat"), None), P("view", ("row", "feat"), None))
    out_specs = (P("view", ("row", "feat"), None), P("view", ("row", "feat"), None))
    return jax.shard_map(
        on_device, mesh=mesh, in_specs=in_specs, out_specs=out_specs, check_vma=False
    )
```

```python
import math

import jax
import jax.numpy as jnp
from jax import lax
from jax.experimental import pallas as pl
from jax.experimental.pallas import tpu as pltpu
from jax.sharding import PartitionSpec as P

ITERS = 2


epsilon = 1e-06
step_rate = 0.5


def xor_move(block, axis, mask):
    count = lax.axis_size(axis)
    return lax.ppermute(block, axis, [(i, i ^ mask) for i in range(count)])


def after(value, *others):
    return lax.optimization_barrier((value,) + others)[0]


def total(values):
    for axis in ("row", "feat"):
        own = values
        for mask in reversed(range(1, lax.axis_size(axis))):
            values = lax.optimization_barrier(values + xor_move(own, axis, mask))
    return values


def join(*blocks):
    return jnp.concatenate(blocks, axis=1)


def split(pair):
    deep = pair.shape[1] // 2
    return pair[:, :deep], pair[:, deep:]


ARRIVALS = (
    ((0, 0), (1, 0), (2, 0), (3, 0), (0, 1), (0, 2)),
    ((0, 3), (3, 2), (1, 1), (1, 2), (2, 1), (2, 2)),
    ((3, 1), (3, 3), (1, 3), (2, 3)),
)


def gather(own):
    b = {(0, 0): own}
    b[0, 2] = xor_move(own, "feat", 2)
    b[0, 1] = xor_move(own, "feat", 1)
    for r in (3, 1, 2):
        b[r, 0] = xor_move(own, "row", r)
    b[3, 2] = xor_move(b[0, 2], "row", 3)
    b[0, 3] = xor_move(b[0, 2], "feat", 1)
    for r in (1, 2):
        pair = join(after(b[0, 1], b[0, 2], b[1, 0]) if r == 1 else b[0, 1], b[0, 2])
        b[r, 1], b[r, 2] = split(xor_move(pair, "row", r))
    b[3, 1], b[3, 3] = split(xor_move(join(b[3, 0], b[3, 2]), "feat", 1))
    for r in (1, 2):
        b[r, 3] = xor_move(b[0, 3], "row", r)
    return b


def scatter(b):
    def send(axis, mask, *blocks):
        half = [block.astype(jnp.bfloat16) for block in blocks]
        got = xor_move(half[0] if len(half) == 1 else join(*half), axis, mask)
        return [part.astype(jnp.float32) for part in (split(got) if len(half) > 1 else [got])]

    def summed(first, *others):
        return lax.optimization_barrier(sum(others, first).astype(jnp.bfloat16))

    near_across, far_across = send("feat", 1, b[3, 1], b[3, 3])
    (left,), (right,) = send("row", 1, b[1, 3]), send("row", 2, b[2, 3])
    ones, twos = zip(*[send("row", r, b[r, 1], b[r, 2]) for r in (1, 2)])
    far_across = summed(b[3, 2], far_across)
    three = summed(after(b[0, 3], far_across), left, right)
    (far_across,), (three,) = send("row", 3, far_across), send("feat", 1, three)
    two = summed(b[0, 2], *twos, far_across, three)
    near_across = summed(after(b[3, 0], two), near_across)
    one = summed(after(b[0, 1], two), *ones)
    (two,), (near_across,), (one,) = (
        send("feat", 2, two),
        send("row", 3, near_across),
        send("feat", 1, one),
    )
    near = b[0, 0] + send("row", 1, b[1, 0])[0] + send("row", 2, b[2, 0])[0]
    return lax.optimization_barrier(near + two) + near_across + one


def any_mesh(samples, own_rows):
    row_total = samples.shape[0] * lax.axis_size("row") * lax.axis_size("feat")
    width_root = math.sqrt(samples.shape[1])
    for sweep in range(ITERS):
        dirs = lax.all_gather(
            own_rows.astype(jnp.bfloat16), ("row", "feat"), axis=0, tiled=True
        )
        summed_proj = jnp.dot(samples, dirs, preferred_element_type=jnp.float32)
        squares = lax.psum(jnp.sum(summed_proj * summed_proj, axis=0), ("row", "feat"))
        scaling = lax.rsqrt(squares / row_total + epsilon)
        own_proj = (summed_proj * scaling).astype(jnp.bfloat16)
        partner_proj = xor_move(own_proj, "view", 1)
        residue = (own_proj.astype(jnp.float32) - partner_proj.astype(jnp.float32)).astype(
            jnp.bfloat16
        )
        share = lax.dot_general(
            samples, residue, (((0,), (0,)), ((), ())), preferred_element_type=jnp.float32
        )
        share = lax.psum_scatter(share, ("row", "feat"), scatter_dimension=0, tiled=True)
        own_rows = width_root * (own_rows * scaling - step_rate * (share / row_total))
    return (own_rows[None], own_proj[None])


def regroup(samples, depth):
    rows_here = samples.shape[0]
    feats = lax.axis_size("feat")
    count = sum(len(places) for places in ARRIVALS)

    def kernel(samples_ref, *refs):
        outs, done = refs[:-1], refs[-1]
        row_at, feat_at = lax.axis_index("row"), lax.axis_index("feat")
        copies = []
        for out, places in zip(outs, ARRIVALS):
            for i, (r, t) in enumerate(places):
                start = pl.multiple_of(((row_at ^ r) * feats + (feat_at ^ t)) * depth, depth)
                copies.append(
                    pltpu.make_async_copy(
                        samples_ref.at[:, pl.ds(start, depth)],
                        out.at[:, pl.ds(i * depth, depth)],
                        done.at[len(copies)],
                    )
                )
                copies[-1].start()
        for copy in copies:
            copy.wait()

    return pl.pallas_call(
        kernel,
        out_shape=[
            jax.ShapeDtypeStruct((rows_here, len(places) * depth), samples.dtype)
            for places in ARRIVALS
        ],
        in_specs=[pl.BlockSpec(memory_space=pl.ANY)],
        out_specs=[pl.BlockSpec(memory_space=pl.ANY) for places in ARRIVALS],
        scratch_shapes=[pltpu.SemaphoreType.DMA((count,))],
        compiler_params=pltpu.CompilerParams(vmem_limit_bytes=44 << 20),
        cost_estimate=pl.CostEstimate(
            flops=0, bytes_accessed=2 * samples.size * 2, transcendentals=0
        ),
        name="regroup",
    )(samples)


def scaled(proj, scaling):
    def kernel(proj_ref, scaling_ref, out_ref):
        columns = proj_ref[...].astype(jnp.float32).T
        out_ref[...] = (columns * scaling_ref[...]).astype(out_ref.dtype)

    return pl.pallas_call(
        kernel,
        out_shape=jax.ShapeDtypeStruct(proj.shape[::-1], proj.dtype),
        in_specs=[pl.BlockSpec(memory_space=pltpu.VMEM)] * 2,
        out_specs=pl.BlockSpec(memory_space=pltpu.VMEM),
        compiler_params=pltpu.CompilerParams(vmem_limit_bytes=8 << 20),
        cost_estimate=pl.CostEstimate(
            flops=proj.size, bytes_accessed=4 * proj.size, transcendentals=0
        ),
        name="scaled",
    )(proj, scaling[None])


def on_device(views, weights):
    samples = views[0]
    own_rows = weights[0]
    rows_here, width = samples.shape
    depth, pairs = own_rows.shape
    rows, feats = lax.axis_size("row"), lax.axis_size("feat")
    if (rows, feats) != (4, 4) or depth % 128:
        return any_mesh(samples, own_rows)
    row_total = rows_here * rows * feats
    width_root = math.sqrt(width)
    groups = regroup(samples, depth)
    dirs_t = own_rows.T
    for sweep in range(ITERS):
        dirs = gather(dirs_t.astype(jnp.bfloat16))
        summed_proj = 0.0
        for g, places in enumerate(ARRIVALS):
            blocks = [dirs[p] for p in places]
            blocks = lax.optimization_barrier(blocks + [dirs[3, 2], dirs[0, 3]])[: len(places)]
            part = lax.dot_general(
                join(*blocks),
                groups[g],
                (((1,), (1,)), ((), ())),
                preferred_element_type=jnp.float32,
            )
            summed_proj = summed_proj + part
            if g < len(ARRIVALS) - 1:
                summed_proj = lax.optimization_barrier(summed_proj)
        kept_proj = lax.optimization_barrier(summed_proj.astype(jnp.bfloat16))
        partner_proj = xor_move(kept_proj, "view", 1).astype(jnp.float32)
        squares = jnp.sum(summed_proj * summed_proj, axis=1)
        scaling = lax.rsqrt(total(squares) / row_total + epsilon)
        partner_scaling = xor_move(scaling, "view", 1)
        own_proj = (kept_proj.astype(jnp.float32) * scaling[:, None]).astype(jnp.bfloat16)
        partner_proj = (partner_proj * partner_scaling[:, None]).astype(jnp.bfloat16)
        residue = (own_proj.astype(jnp.float32) - partner_proj.astype(jnp.float32)).astype(
            jnp.bfloat16
        )
        shares = {}
        for g in (2, 1, 0):
            share = lax.dot_general(
                residue, groups[g], (((1,), (0,)), ((), ())), preferred_element_type=jnp.float32
            )
            for i, place in enumerate(ARRIVALS[g]):
                shares[place] = share[:, i * depth : (i + 1) * depth]
        if sweep == ITERS - 1:
            shown = scaled(kept_proj, scaling)
        grad = scatter(shares) / row_total
        dirs_t = width_root * (dirs_t * scaling[:, None] - step_rate * grad)
    return (dirs_t.T[None], shown[None])


def solution(mesh):
    in_specs = (P("view", ("row", "feat"), None), P("view", ("row", "feat"), None))
    out_specs = (P("view", ("row", "feat"), None), P("view", ("row", "feat"), None))
    return jax.shard_map(
        on_device, mesh=mesh, in_specs=in_specs, out_specs=out_specs, check_vma=False
    )
```

```python
import math

import jax
import jax.numpy as jnp
from jax import lax
from jax.experimental import pallas as pl
from jax.experimental.pallas import tpu as pltpu
from jax.sharding import PartitionSpec as P

ITERS = 2


epsilon = 1e-06
step_rate = 0.5


def xor_move(block, axis, mask):
    count = lax.axis_size(axis)
    return lax.ppermute(block, axis, [(i, i ^ mask) for i in range(count)])


def after(value, *others):
    return lax.optimization_barrier((value,) + others)[0]


def total(values):
    for axis in ("row", "feat"):
        own = values
        for mask in reversed(range(1, lax.axis_size(axis))):
            values = lax.optimization_barrier(values + xor_move(own, axis, mask))
    return values


def join(*blocks):
    return jnp.concatenate(blocks, axis=1)


def split(pair):
    deep = pair.shape[1] // 2
    return pair[:, :deep], pair[:, deep:]


ARRIVALS = (
    ((0, 0), (1, 0), (3, 0), (0, 1), (0, 2)),
    ((2, 0), (0, 3), (3, 2), (1, 1), (1, 2), (2, 1), (2, 2)),
    ((3, 1), (3, 3), (1, 3), (2, 3)),
)


def gather(own):
    b = {(0, 0): own}
    b[0, 2] = xor_move(own, "feat", 2)
    b[0, 1] = xor_move(own, "feat", 1)
    for r in (3, 1, 2):
        b[r, 0] = xor_move(own, "row", r)
    b[3, 2] = xor_move(b[0, 2], "row", 3)
    b[0, 3] = xor_move(b[0, 2], "feat", 1)
    for r in (1, 2):
        pair = join(after(b[0, 1], b[0, 2], b[1, 0]) if r == 1 else b[0, 1], b[0, 2])
        b[r, 1], b[r, 2] = split(xor_move(pair, "row", r))
    b[3, 1], b[3, 3] = split(xor_move(join(b[3, 0], b[3, 2]), "feat", 1))
    for r in (1, 2):
        b[r, 3] = xor_move(b[0, 3], "row", r)
    return b


def scatter(b):
    def send(axis, mask, *blocks):
        half = [block.astype(jnp.bfloat16) for block in blocks]
        got = xor_move(half[0] if len(half) == 1 else join(*half), axis, mask)
        return [part.astype(jnp.float32) for part in (split(got) if len(half) > 1 else [got])]

    def summed(first, *others):
        return lax.optimization_barrier(sum(others, first).astype(jnp.bfloat16))

    near_across, far_across = send("feat", 1, b[3, 1], b[3, 3])
    (left,), (right,) = send("row", 1, b[1, 3]), send("row", 2, b[2, 3])
    ones, twos = zip(*[send("row", r, b[r, 1], b[r, 2]) for r in (1, 2)])
    far_across = summed(b[3, 2], far_across)
    three = summed(after(b[0, 3], far_across), left, right)
    (far_across,), (three,) = send("row", 3, far_across), send("feat", 1, three)
    two = summed(b[0, 2], *twos, far_across, three)
    near_across = summed(after(b[3, 0], two), near_across)
    one = summed(after(b[0, 1], two), *ones)
    (two,), (near_across,), (one,) = (
        send("feat", 2, two),
        send("row", 3, near_across),
        send("feat", 1, one),
    )
    near = b[0, 0] + send("row", 1, b[1, 0])[0] + send("row", 2, b[2, 0])[0]
    return lax.optimization_barrier(near + two) + near_across + one


def any_mesh(samples, own_rows):
    row_total = samples.shape[0] * lax.axis_size("row") * lax.axis_size("feat")
    width_root = math.sqrt(samples.shape[1])
    for sweep in range(ITERS):
        dirs = lax.all_gather(
            own_rows.astype(jnp.bfloat16), ("row", "feat"), axis=0, tiled=True
        )
        summed_proj = jnp.dot(samples, dirs, preferred_element_type=jnp.float32)
        squares = lax.psum(jnp.sum(summed_proj * summed_proj, axis=0), ("row", "feat"))
        scaling = lax.rsqrt(squares / row_total + epsilon)
        own_proj = (summed_proj * scaling).astype(jnp.bfloat16)
        partner_proj = xor_move(own_proj, "view", 1)
        residue = (own_proj.astype(jnp.float32) - partner_proj.astype(jnp.float32)).astype(
            jnp.bfloat16
        )
        share = lax.dot_general(
            samples, residue, (((0,), (0,)), ((), ())), preferred_element_type=jnp.float32
        )
        share = lax.psum_scatter(share, ("row", "feat"), scatter_dimension=0, tiled=True)
        own_rows = width_root * (own_rows * scaling - step_rate * (share / row_total))
    return (own_rows[None], own_proj[None])


def regroup(samples, depth):
    rows_here = samples.shape[0]
    feats = lax.axis_size("feat")
    count = sum(len(places) for places in ARRIVALS)

    def kernel(samples_ref, *refs):
        outs, done = refs[:-1], refs[-1]
        row_at, feat_at = lax.axis_index("row"), lax.axis_index("feat")
        copies = []
        for out, places in zip(outs, ARRIVALS):
            for i, (r, t) in enumerate(places):
                start = pl.multiple_of(((row_at ^ r) * feats + (feat_at ^ t)) * depth, depth)
                copies.append(
                    pltpu.make_async_copy(
                        samples_ref.at[:, pl.ds(start, depth)],
                        out.at[:, pl.ds(i * depth, depth)],
                        done.at[len(copies)],
                    )
                )
                copies[-1].start()
        for copy in copies:
            copy.wait()

    return pl.pallas_call(
        kernel,
        out_shape=[
            jax.ShapeDtypeStruct((rows_here, len(places) * depth), samples.dtype)
            for places in ARRIVALS
        ],
        in_specs=[pl.BlockSpec(memory_space=pl.ANY)],
        out_specs=[pl.BlockSpec(memory_space=pl.ANY) for places in ARRIVALS],
        scratch_shapes=[pltpu.SemaphoreType.DMA((count,))],
        compiler_params=pltpu.CompilerParams(vmem_limit_bytes=44 << 20),
        cost_estimate=pl.CostEstimate(
            flops=0, bytes_accessed=2 * samples.size * 2, transcendentals=0
        ),
        name="regroup",
    )(samples)


def scaled(proj, scaling):
    def kernel(proj_ref, scaling_ref, out_ref):
        columns = proj_ref[...].astype(jnp.float32).T
        out_ref[...] = (columns * scaling_ref[...]).astype(out_ref.dtype)

    return pl.pallas_call(
        kernel,
        out_shape=jax.ShapeDtypeStruct(proj.shape[::-1], proj.dtype),
        in_specs=[pl.BlockSpec(memory_space=pltpu.VMEM)] * 2,
        out_specs=pl.BlockSpec(memory_space=pltpu.VMEM),
        compiler_params=pltpu.CompilerParams(vmem_limit_bytes=8 << 20),
        cost_estimate=pl.CostEstimate(
            flops=proj.size, bytes_accessed=4 * proj.size, transcendentals=0
        ),
        name="scaled",
    )(proj, scaling[None])


def on_device(views, weights):
    samples = views[0]
    own_rows = weights[0]
    rows_here, width = samples.shape
    depth, pairs = own_rows.shape
    rows, feats = lax.axis_size("row"), lax.axis_size("feat")
    if (rows, feats) != (4, 4) or depth % 128:
        return any_mesh(samples, own_rows)
    row_total = rows_here * rows * feats
    width_root = math.sqrt(width)
    groups = regroup(samples, depth)
    dirs_t = own_rows.T
    for sweep in range(ITERS):
        dirs = gather(dirs_t.astype(jnp.bfloat16))
        summed_proj = 0.0
        for g, places in enumerate(ARRIVALS):
            blocks = [dirs[p] for p in places]
            blocks = lax.optimization_barrier(blocks + [dirs[3, 2], dirs[0, 3]])[: len(places)]
            part = lax.dot_general(
                join(*blocks),
                groups[g],
                (((1,), (1,)), ((), ())),
                preferred_element_type=jnp.float32,
            )
            summed_proj = summed_proj + part
            if g < len(ARRIVALS) - 1:
                summed_proj = lax.optimization_barrier(summed_proj)
        kept_proj = lax.optimization_barrier(summed_proj.astype(jnp.bfloat16))
        partner_proj = xor_move(kept_proj, "view", 1).astype(jnp.float32)
        squares = jnp.sum(summed_proj * summed_proj, axis=1)
        scaling = lax.rsqrt(total(squares) / row_total + epsilon)
        partner_scaling = xor_move(scaling, "view", 1)
        own_proj = (kept_proj.astype(jnp.float32) * scaling[:, None]).astype(jnp.bfloat16)
        partner_proj = (partner_proj * partner_scaling[:, None]).astype(jnp.bfloat16)
        residue = (own_proj.astype(jnp.float32) - partner_proj.astype(jnp.float32)).astype(
            jnp.bfloat16
        )
        shares = {}
        for g in (2, 1, 0):
            share = lax.dot_general(
                residue, groups[g], (((1,), (0,)), ((), ())), preferred_element_type=jnp.float32
            )
            for i, place in enumerate(ARRIVALS[g]):
                shares[place] = share[:, i * depth : (i + 1) * depth]
        if sweep == ITERS - 1:
            shown = scaled(kept_proj, scaling)
        grad = scatter(shares) / row_total
        dirs_t = width_root * (dirs_t * scaling[:, None] - step_rate * grad)
    return (dirs_t.T[None], shown[None])


def solution(mesh):
    in_specs = (P("view", ("row", "feat"), None), P("view", ("row", "feat"), None))
    out_specs = (P("view", ("row", "feat"), None), P("view", ("row", "feat"), None))
    return jax.shard_map(
        on_device, mesh=mesh, in_specs=in_specs, out_specs=out_specs, check_vma=False
    )
```

```python
import math

import jax
import jax.numpy as jnp
from jax import lax
from jax.experimental import pallas as pl
from jax.experimental.pallas import tpu as pltpu
from jax.sharding import PartitionSpec as P

ITERS = 2


epsilon = 1e-06
step_rate = 0.5


def xor_move(block, axis, mask):
    count = lax.axis_size(axis)
    return lax.ppermute(block, axis, [(i, i ^ mask) for i in range(count)])


def after(value, *others):
    return lax.optimization_barrier((value,) + others)[0]


def total(values):
    for axis in ("row", "feat"):
        own = values
        for mask in reversed(range(1, lax.axis_size(axis))):
            values = lax.optimization_barrier(values + xor_move(own, axis, mask))
    return values


def join(*blocks):
    return jnp.concatenate(blocks, axis=1)


def split(pair):
    deep = pair.shape[1] // 2
    return pair[:, :deep], pair[:, deep:]


ARRIVALS = (
    ((0, 0), (1, 0), (2, 0), (3, 0), (0, 1), (0, 2)),
    ((0, 3), (3, 2), (1, 1), (1, 2), (2, 1), (2, 2)),
    ((3, 1), (3, 3), (1, 3), (2, 3)),
)


def gather(own):
    b = {(0, 0): own}
    b[0, 2] = xor_move(own, "feat", 2)
    b[0, 1] = xor_move(own, "feat", 1)
    for r in (3, 1, 2):
        b[r, 0] = xor_move(own, "row", r)
    b[3, 2] = xor_move(b[0, 2], "row", 3)
    b[0, 3] = xor_move(b[0, 2], "feat", 1)
    for r in (1, 2):
        pair = join(after(b[0, 1], b[0, 2], b[1, 0]) if r == 1 else b[0, 1], b[0, 2])
        b[r, 1], b[r, 2] = split(xor_move(pair, "row", r))
    b[3, 1], b[3, 3] = split(xor_move(join(b[3, 0], b[3, 2]), "feat", 1))
    for r in (1, 2):
        b[r, 3] = xor_move(b[0, 3], "row", r)
    return b


def scatter(b):
    def send(axis, mask, *blocks):
        half = [block.astype(jnp.bfloat16) for block in blocks]
        got = xor_move(half[0] if len(half) == 1 else join(*half), axis, mask)
        return [part.astype(jnp.float32) for part in (split(got) if len(half) > 1 else [got])]

    def summed(first, *others):
        return lax.optimization_barrier(sum(others, first).astype(jnp.bfloat16))

    near_across, far_across = send("feat", 1, b[3, 1], b[3, 3])
    (left,), (right,) = send("row", 1, b[1, 3]), send("row", 2, b[2, 3])
    ones, twos = zip(*[send("row", r, b[r, 1], b[r, 2]) for r in (1, 2)])
    far_across = summed(b[3, 2], far_across)
    three = summed(after(b[0, 3], far_across), left, right)
    (far_across,), (three,) = send("row", 3, far_across), send("feat", 1, three)
    two = summed(b[0, 2], *twos, far_across, three)
    near_across = summed(after(b[3, 0], two), near_across)
    one = summed(after(b[0, 1], three), *ones)
    (two,), (near_across,), (one,) = (
        send("feat", 2, two),
        send("row", 3, near_across),
        send("feat", 1, one),
    )
    near = b[0, 0] + send("row", 1, b[1, 0])[0] + send("row", 2, b[2, 0])[0]
    return lax.optimization_barrier(near + two) + near_across + one


def any_mesh(samples, own_rows):
    row_total = samples.shape[0] * lax.axis_size("row") * lax.axis_size("feat")
    width_root = math.sqrt(samples.shape[1])
    for sweep in range(ITERS):
        dirs = lax.all_gather(
            own_rows.astype(jnp.bfloat16), ("row", "feat"), axis=0, tiled=True
        )
        summed_proj = jnp.dot(samples, dirs, preferred_element_type=jnp.float32)
        squares = lax.psum(jnp.sum(summed_proj * summed_proj, axis=0), ("row", "feat"))
        scaling = lax.rsqrt(squares / row_total + epsilon)
        own_proj = (summed_proj * scaling).astype(jnp.bfloat16)
        partner_proj = xor_move(own_proj, "view", 1)
        residue = (own_proj.astype(jnp.float32) - partner_proj.astype(jnp.float32)).astype(
            jnp.bfloat16
        )
        share = lax.dot_general(
            samples, residue, (((0,), (0,)), ((), ())), preferred_element_type=jnp.float32
        )
        share = lax.psum_scatter(share, ("row", "feat"), scatter_dimension=0, tiled=True)
        own_rows = width_root * (own_rows * scaling - step_rate * (share / row_total))
    return (own_rows[None], own_proj[None])


def regroup(samples, depth):
    rows_here = samples.shape[0]
    feats = lax.axis_size("feat")
    count = sum(len(places) for places in ARRIVALS)

    def kernel(samples_ref, *refs):
        outs, done = refs[:-1], refs[-1]
        row_at, feat_at = lax.axis_index("row"), lax.axis_index("feat")
        copies = []
        for out, places in zip(outs, ARRIVALS):
            for i, (r, t) in enumerate(places):
                start = pl.multiple_of(((row_at ^ r) * feats + (feat_at ^ t)) * depth, depth)
                copies.append(
                    pltpu.make_async_copy(
                        samples_ref.at[:, pl.ds(start, depth)],
                        out.at[:, pl.ds(i * depth, depth)],
                        done.at[len(copies)],
                    )
                )
                copies[-1].start()
        for copy in copies:
            copy.wait()

    return pl.pallas_call(
        kernel,
        out_shape=[
            jax.ShapeDtypeStruct((rows_here, len(places) * depth), samples.dtype)
            for places in ARRIVALS
        ],
        in_specs=[pl.BlockSpec(memory_space=pl.ANY)],
        out_specs=[pl.BlockSpec(memory_space=pl.ANY) for places in ARRIVALS],
        scratch_shapes=[pltpu.SemaphoreType.DMA((count,))],
        compiler_params=pltpu.CompilerParams(vmem_limit_bytes=44 << 20),
        cost_estimate=pl.CostEstimate(
            flops=0, bytes_accessed=2 * samples.size * 2, transcendentals=0
        ),
        name="regroup",
    )(samples)


def scaled(proj, scaling):
    def kernel(proj_ref, scaling_ref, out_ref):
        columns = proj_ref[...].astype(jnp.float32).T
        out_ref[...] = (columns * scaling_ref[...]).astype(out_ref.dtype)

    return pl.pallas_call(
        kernel,
        out_shape=jax.ShapeDtypeStruct(proj.shape[::-1], proj.dtype),
        in_specs=[pl.BlockSpec(memory_space=pltpu.VMEM)] * 2,
        out_specs=pl.BlockSpec(memory_space=pltpu.VMEM),
        compiler_params=pltpu.CompilerParams(vmem_limit_bytes=8 << 20),
        cost_estimate=pl.CostEstimate(
            flops=proj.size, bytes_accessed=4 * proj.size, transcendentals=0
        ),
        name="scaled",
    )(proj, scaling[None])


def on_device(views, weights):
    samples = views[0]
    own_rows = weights[0]
    rows_here, width = samples.shape
    depth, pairs = own_rows.shape
    rows, feats = lax.axis_size("row"), lax.axis_size("feat")
    if (rows, feats) != (4, 4) or depth % 128:
        return any_mesh(samples, own_rows)
    row_total = rows_here * rows * feats
    width_root = math.sqrt(width)
    groups = regroup(samples, depth)
    dirs_t = own_rows.T
    for sweep in range(ITERS):
        dirs = gather(dirs_t.astype(jnp.bfloat16))
        summed_proj = 0.0
        for g, places in enumerate(ARRIVALS):
            blocks = [dirs[p] for p in places]
            blocks = lax.optimization_barrier(blocks + [dirs[3, 2], dirs[0, 3]])[: len(places)]
            part = lax.dot_general(
                join(*blocks),
                groups[g],
                (((1,), (1,)), ((), ())),
                preferred_element_type=jnp.float32,
            )
            summed_proj = summed_proj + part
            if g < len(ARRIVALS) - 1:
                summed_proj = lax.optimization_barrier(summed_proj)
        kept_proj = lax.optimization_barrier(summed_proj.astype(jnp.bfloat16))
        partner_proj = xor_move(kept_proj, "view", 1).astype(jnp.float32)
        squares = jnp.sum(summed_proj * summed_proj, axis=1)
        scaling = lax.rsqrt(total(squares) / row_total + epsilon)
        partner_scaling = xor_move(scaling, "view", 1)
        own_proj = (kept_proj.astype(jnp.float32) * scaling[:, None]).astype(jnp.bfloat16)
        partner_proj = (partner_proj * partner_scaling[:, None]).astype(jnp.bfloat16)
        residue = (own_proj.astype(jnp.float32) - partner_proj.astype(jnp.float32)).astype(
            jnp.bfloat16
        )
        shares = {}
        for g in (2, 1, 0):
            share = lax.dot_general(
                residue, groups[g], (((1,), (0,)), ((), ())), preferred_element_type=jnp.float32
            )
            for i, place in enumerate(ARRIVALS[g]):
                shares[place] = share[:, i * depth : (i + 1) * depth]
        if sweep == ITERS - 1:
            shown = scaled(kept_proj, scaling)
        grad = scatter(shares) / row_total
        dirs_t = width_root * (dirs_t * scaling[:, None] - step_rate * grad)
    return (dirs_t.T[None], shown[None])


def solution(mesh):
    in_specs = (P("view", ("row", "feat"), None), P("view", ("row", "feat"), None))
    out_specs = (P("view", ("row", "feat"), None), P("view", ("row", "feat"), None))
    return jax.shard_map(
        on_device, mesh=mesh, in_specs=in_specs, out_specs=out_specs, check_vma=False
    )
```

```python
import math

import jax
import jax.numpy as jnp
from jax import lax
from jax.experimental import pallas as pl
from jax.experimental.pallas import tpu as pltpu
from jax.sharding import PartitionSpec as P

ITERS = 2


epsilon = 1e-06
step_rate = 0.5


def xor_move(block, axis, mask):
    count = lax.axis_size(axis)
    return lax.ppermute(block, axis, [(i, i ^ mask) for i in range(count)])


def after(value, *others):
    return lax.optimization_barrier((value,) + others)[0]


def total(values):
    for axis in ("row", "feat"):
        own = values
        masks = sorted(range(1, lax.axis_size(axis)), reverse=True)
        if axis == "feat":
            masks.sort(key=lambda mask: mask != lax.axis_size(axis) // 2)
        for mask in masks:
            values = lax.optimization_barrier(values + xor_move(own, axis, mask))
    return values


def join(*blocks):
    return jnp.concatenate(blocks, axis=1)


def split(pair):
    deep = pair.shape[1] // 2
    return pair[:, :deep], pair[:, deep:]


ARRIVALS = (
    ((0, 0), (1, 0), (2, 0), (3, 0), (0, 1), (0, 2)),
    ((0, 3), (3, 2), (1, 1), (1, 2), (2, 1), (2, 2)),
    ((3, 1), (3, 3), (1, 3), (2, 3)),
)


def gather(own):
    b = {(0, 0): own}
    b[0, 2] = xor_move(own, "feat", 2)
    b[0, 1] = xor_move(own, "feat", 1)
    for r in (3, 1, 2):
        b[r, 0] = xor_move(own, "row", r)
    b[3, 2] = xor_move(b[0, 2], "row", 3)
    b[0, 3] = xor_move(b[0, 2], "feat", 1)
    for r in (1, 2):
        pair = join(after(b[0, 1], b[0, 2], b[1, 0]) if r == 1 else b[0, 1], b[0, 2])
        b[r, 1], b[r, 2] = split(xor_move(pair, "row", r))
    b[3, 1], b[3, 3] = split(xor_move(join(b[3, 0], b[3, 2]), "feat", 1))
    for r in (1, 2):
        b[r, 3] = xor_move(b[0, 3], "row", r)
    return b


def scatter(b):
    def send(axis, mask, *blocks):
        half = [block.astype(jnp.bfloat16) for block in blocks]
        got = xor_move(half[0] if len(half) == 1 else join(*half), axis, mask)
        return [part.astype(jnp.float32) for part in (split(got) if len(half) > 1 else [got])]

    def summed(first, *others):
        return lax.optimization_barrier(sum(others, first).astype(jnp.bfloat16))

    near_across, far_across = send("feat", 1, b[3, 1], b[3, 3])
    (left,), (right,) = send("row", 1, b[1, 3]), send("row", 2, b[2, 3])
    ones, twos = zip(*[send("row", r, b[r, 1], b[r, 2]) for r in (1, 2)])
    far_across = summed(b[3, 2], far_across)
    three = summed(after(b[0, 3], far_across), left, right)
    (far_across,), (three,) = send("row", 3, far_across), send("feat", 1, three)
    two = summed(b[0, 2], *twos, far_across, three)
    near_across = summed(after(b[3, 0], two), near_across)
    one = summed(after(b[0, 1], two), *ones)
    (two,), (near_across,), (one,) = (
        send("feat", 2, two),
        send("row", 3, near_across),
        send("feat", 1, one),
    )
    near = b[0, 0] + send("row", 1, b[1, 0])[0] + send("row", 2, b[2, 0])[0]
    return lax.optimization_barrier(near + two) + near_across + one


def any_mesh(samples, own_rows):
    row_total = samples.shape[0] * lax.axis_size("row") * lax.axis_size("feat")
    width_root = math.sqrt(samples.shape[1])
    for sweep in range(ITERS):
        dirs = lax.all_gather(
            own_rows.astype(jnp.bfloat16), ("row", "feat"), axis=0, tiled=True
        )
        summed_proj = jnp.dot(samples, dirs, preferred_element_type=jnp.float32)
        squares = lax.psum(jnp.sum(summed_proj * summed_proj, axis=0), ("row", "feat"))
        scaling = lax.rsqrt(squares / row_total + epsilon)
        own_proj = (summed_proj * scaling).astype(jnp.bfloat16)
        partner_proj = xor_move(own_proj, "view", 1)
        residue = (own_proj.astype(jnp.float32) - partner_proj.astype(jnp.float32)).astype(
            jnp.bfloat16
        )
        share = lax.dot_general(
            samples, residue, (((0,), (0,)), ((), ())), preferred_element_type=jnp.float32
        )
        share = lax.psum_scatter(share, ("row", "feat"), scatter_dimension=0, tiled=True)
        own_rows = width_root * (own_rows * scaling - step_rate * (share / row_total))
    return (own_rows[None], own_proj[None])


def regroup(samples, depth):
    rows_here = samples.shape[0]
    feats = lax.axis_size("feat")
    count = sum(len(places) for places in ARRIVALS)

    def kernel(samples_ref, *refs):
        outs, done = refs[:-1], refs[-1]
        row_at, feat_at = lax.axis_index("row"), lax.axis_index("feat")
        copies = []
        for out, places in zip(outs, ARRIVALS):
            for i, (r, t) in enumerate(places):
                start = pl.multiple_of(((row_at ^ r) * feats + (feat_at ^ t)) * depth, depth)
                copies.append(
                    pltpu.make_async_copy(
                        samples_ref.at[:, pl.ds(start, depth)],
                        out.at[:, pl.ds(i * depth, depth)],
                        done.at[len(copies)],
                    )
                )
                copies[-1].start()
        for copy in copies:
            copy.wait()

    return pl.pallas_call(
        kernel,
        out_shape=[
            jax.ShapeDtypeStruct((rows_here, len(places) * depth), samples.dtype)
            for places in ARRIVALS
        ],
        in_specs=[pl.BlockSpec(memory_space=pl.ANY)],
        out_specs=[pl.BlockSpec(memory_space=pl.ANY) for places in ARRIVALS],
        scratch_shapes=[pltpu.SemaphoreType.DMA((count,))],
        compiler_params=pltpu.CompilerParams(vmem_limit_bytes=44 << 20),
        cost_estimate=pl.CostEstimate(
            flops=0, bytes_accessed=2 * samples.size * 2, transcendentals=0
        ),
        name="regroup",
    )(samples)


def scaled(proj, scaling):
    def kernel(proj_ref, scaling_ref, out_ref):
        columns = proj_ref[...].astype(jnp.float32).T
        out_ref[...] = (columns * scaling_ref[...]).astype(out_ref.dtype)

    return pl.pallas_call(
        kernel,
        out_shape=jax.ShapeDtypeStruct(proj.shape[::-1], proj.dtype),
        in_specs=[pl.BlockSpec(memory_space=pltpu.VMEM)] * 2,
        out_specs=pl.BlockSpec(memory_space=pltpu.VMEM),
        compiler_params=pltpu.CompilerParams(vmem_limit_bytes=8 << 20),
        cost_estimate=pl.CostEstimate(
            flops=proj.size, bytes_accessed=4 * proj.size, transcendentals=0
        ),
        name="scaled",
    )(proj, scaling[None])


def on_device(views, weights):
    samples = views[0]
    own_rows = weights[0]
    rows_here, width = samples.shape
    depth, pairs = own_rows.shape
    rows, feats = lax.axis_size("row"), lax.axis_size("feat")
    if (rows, feats) != (4, 4) or depth % 128:
        return any_mesh(samples, own_rows)
    row_total = rows_here * rows * feats
    width_root = math.sqrt(width)
    groups = regroup(samples, depth)
    dirs_t = own_rows.T
    for sweep in range(ITERS):
        dirs = gather(dirs_t.astype(jnp.bfloat16))
        summed_proj = 0.0
        for g, places in enumerate(ARRIVALS):
            blocks = [dirs[p] for p in places]
            blocks = lax.optimization_barrier(blocks + [dirs[3, 2], dirs[0, 3]])[: len(places)]
            part = lax.dot_general(
                join(*blocks),
                groups[g],
                (((1,), (1,)), ((), ())),
                preferred_element_type=jnp.float32,
            )
            summed_proj = summed_proj + part
            if g < len(ARRIVALS) - 1:
                summed_proj = lax.optimization_barrier(summed_proj)
        kept_proj = lax.optimization_barrier(summed_proj.astype(jnp.bfloat16))
        partner_proj = xor_move(kept_proj, "view", 1).astype(jnp.float32)
        squares = jnp.sum(summed_proj * summed_proj, axis=1)
        scaling = lax.rsqrt(total(squares) / row_total + epsilon)
        partner_scaling = xor_move(scaling, "view", 1)
        own_proj = (kept_proj.astype(jnp.float32) * scaling[:, None]).astype(jnp.bfloat16)
        partner_proj = (partner_proj * partner_scaling[:, None]).astype(jnp.bfloat16)
        residue = (own_proj.astype(jnp.float32) - partner_proj.astype(jnp.float32)).astype(
            jnp.bfloat16
        )
        shares = {}
        for g in (2, 1, 0):
            share = lax.dot_general(
                residue, groups[g], (((1,), (0,)), ((), ())), preferred_element_type=jnp.float32
            )
            for i, place in enumerate(ARRIVALS[g]):
                shares[place] = share[:, i * depth : (i + 1) * depth]
        if sweep == ITERS - 1:
            shown = scaled(kept_proj, scaling)
        grad = scatter(shares) / row_total
        dirs_t = width_root * (dirs_t * scaling[:, None] - step_rate * grad)
    return (dirs_t.T[None], shown[None])


def solution(mesh):
    in_specs = (P("view", ("row", "feat"), None), P("view", ("row", "feat"), None))
    out_specs = (P("view", ("row", "feat"), None), P("view", ("row", "feat"), None))
    return jax.shard_map(
        on_device, mesh=mesh, in_specs=in_specs, out_specs=out_specs, check_vma=False
    )
```
